32 devices in a mesh: axial: 8 (over z, x), azim: 2 (over y), bank: 2 (over core).
Axes of the slice: x: 2, y: 2, z: 4, core: 2. Of those that a mesh axis runs over, the one named last changes fastest.
Arguments:
- adjoint_state: float32 [2, 64, 64, 512], P('bank', None, 'axial', 'azim'), may hold values from -6 to 6
- adjoint_source: float32 [2, 64, 64, 512], P('bank', None, 'axial', 'azim'), may hold values from -6 to 6
- reaction_rate: float32 [2, 64, 512], P('bank', 'axial', 'azim'), may hold values from 0.5 to 2
- jacobian: float32 [2, 64, 64], P('bank'), may hold values from -0.75 to 0.75
- lifting: float32 [2, 6, 64, 512], P('bank', None, 'axial', 'azim'), may hold values from -0.125 to 0.125
- separator: int32 [8, 2, 2, 6], P('axial', 'azim', 'bank'), may hold values from 0 to 2047
- leaf_schur: float32 [8, 2, 2, 384, 384], P('axial', 'azim', 'bank'), may hold values from -14 to 43, as said below
Outputs:
- interface_adjoint: float32 [8, 2, 2, 384], P('axial', 'azim', 'bank')
The draws below stay inside these ranges and needn't reach their ends.
Inputs may be any that keep to these rules, and one draw needn't show every extreme that they name: `separator`: a cell k = row * 256 + column of the device's own block. `leaf_schur`: every leaf block is symmetric positive definite.
All inputs are finite; a program needn't handle non-finite values.
Results may differ from the reference program's by a relative error of at most 0.0003.
Values sent between devices are 32-bit elements; how exact they have to be, the bound alone decides.
No kernel may reach another device: no remote copies, remote signals or barrier semaphores. Data moves between devices by JAX's collectives and lax.ppermute only.
A program may use at most 64 MiB of HBM per device.

```python
import math
import jax
import jax.numpy as jnp
from jax import lax

NVAR = 64
SEP = 6
CX = 8
CZ = 256
W = 384
NAX = 64
NAZ = 512
N_AXIAL = 8
N_AZIM = 2
N_BANK = 2


def draw_leaf_schur(key, part):
    key_rate, key_shift = jax.random.split(key)
    full_shape = (N_AXIAL, N_AZIM, N_BANK, W, W)
    rows = lax.broadcasted_iota(jnp.int32, (W, W), 0)
    cols = lax.broadcasted_iota(jnp.int32, (W, W), 1)
    distance = jnp.abs(rows - cols)
    kernel = jnp.ones((W, W), jnp.float32)
    for level in range(16):
        kernel = kernel * jnp.where(distance - 1 >= 1 << level, 0.25, 1.0).astype(jnp.float32)
    levels = jax.random.randint(key_rate, full_shape, 4, 13)
    shift = jnp.exp(jax.random.uniform(key_shift, full_shape[:-1], jnp.float32, jnp.log(0.01), jnp.log(0.08)))
    rates = levels.astype(jnp.float32) * 0.125
    rates = jnp.where(rows < cols, rates, jnp.swapaxes(rates, -1, -2))
    offdiag = jnp.where(distance > 0, rates * kernel, 0.0)
    row_total = jnp.sum(offdiag, axis=-1)
    diagonal = row_total + shift
    return 8.0 * jnp.where(distance == 0, diagonal[..., None], -offdiag)


def place_ends(entries, rng, smallest, largest):
    extent = entries.shape
    spot = [jax.random.randint(jax.random.fold_in(rng, axis), (), 0, extent[axis]) for axis in range(len(extent))]
    entries = entries.at[tuple(spot)].set(smallest)
    longest = extent.index(max(extent))
    spot[longest] = (spot[longest] + 1) % extent[longest]
    return entries.at[tuple(spot)].set(largest)


def shard_levels(rng, dims, cuts, least, largest):
    def one(dim, blocks):
        steps = jax.random.uniform(jax.random.fold_in(jax.random.fold_in(rng, 6), dim), (blocks,), jnp.float32, least / len(cuts), largest / len(cuts))
        return jnp.repeat(jnp.exp(steps), dims[dim] // blocks).reshape((-1,) + (1,) * (len(dims) - dim - 1))

    factor_of = one(*cuts[0])
    for cut in cuts[1:]:
        factor_of = factor_of * one(*cut)
    return factor_of


def centred(rng, dims, scale, reach, pieces=(), dtype=jnp.bfloat16):
    gain = shard_levels(rng, dims, pieces, -0.22, 0.18) if pieces else 1.0
    drawn = jax.random.normal(rng, dims, jnp.float32) * scale * gain
    return jnp.minimum(jnp.maximum(drawn, -reach), reach).astype(dtype)


def setup_inputs(seed: int = 0) -> dict:
    keys = jax.random.split(jax.random.key(seed), 8)
    return {
        "adjoint_state": centred(keys[0], (N_BANK, NVAR, NAX, NAZ), 1.0, 6.0, ((0, 2), (2, 8), (3, 2)), jnp.float32),
        "adjoint_source": centred(keys[1], (N_BANK, NVAR, NAX, NAZ), 1.0, 6.0, ((0, 2), (2, 8), (3, 2)), jnp.float32),
        "reaction_rate": jnp.clip(jnp.exp(math.log(2.0) - 1.3862944 * jax.random.uniform(keys[2], (N_BANK, NAX, NAZ), jnp.float32) ** shard_levels(keys[2], (N_BANK, NAX, NAZ), ((0, 2), (1, 8), (2, 2)), -0.2, 0.2)), 0.5, 2.0),
        "jacobian": centred(keys[3], (N_BANK, NVAR, NVAR), NVAR ** -0.5, 0.75, ((0, 2),), jnp.float32),
        "lifting": centred(keys[4], (N_BANK, SEP, NAX, NAZ), (CX * CZ) ** -0.5, 0.125, ((0, 2), (2, 8), (3, 2)), jnp.float32),
        "separator": place_ends(jax.random.randint(keys[5], (N_AXIAL, N_AZIM, N_BANK, SEP), 0, CX * CZ), jax.random.fold_in(keys[5], 1), 0, (CX * CZ) - 1).astype(jnp.int32),
        "leaf_schur": draw_leaf_schur(jax.random.fold_in(keys[7], 71), 0),
    }


highest = lax.Precision.HIGHEST
diffusion = 0.5

def residual_field(adjoint_state, adjoint_source, reaction_rate, jacobian):
    scaled = reaction_rate[:, None] * adjoint_state
    reaction = jnp.einsum('bvu,bvxz->buxz', jacobian, scaled, precision=highest)
    padded = jnp.pad(adjoint_state, ((0, 0), (0, 0), (1, 1), (0, 0)))
    neighbours = padded[:, :, 2:, :] + padded[:, :, :-2, :]
    neighbours = neighbours + jnp.roll(adjoint_state, 1, axis=3) + jnp.roll(adjoint_state, -1, axis=3)
    return adjoint_source - reaction - diffusion * (4.0 * adjoint_state - neighbours)

def to_blocks(values):
    chans = values.shape[1]
    shaped = values.reshape(N_BANK, chans, N_AXIAL, CX, N_AZIM, CZ)
    shaped = jnp.transpose(shaped, (2, 4, 0, 1, 3, 5))
    return shaped.reshape(N_AXIAL, N_AZIM, N_BANK, chans, CX * CZ)

def eliminate(first_shared, second_shared, shared_rhs, middle):
    shared_sum = first_shared[:, middle:] + second_shared[:, middle:]
    factor = jnp.linalg.cholesky(shared_sum)
    coupling = jnp.concatenate([first_shared[:, :middle], second_shared[:, :middle]], axis=1)
    inner = jax.scipy.linalg.solve_triangular(factor, coupling, lower=True)
    coupled = jax.scipy.linalg.solve_triangular(factor, inner, lower=True, trans=1)
    inner_rhs = jax.scipy.linalg.solve_triangular(factor, shared_rhs, lower=True)
    shifted = jax.scipy.linalg.solve_triangular(factor, inner_rhs, lower=True, trans=1)
    return (coupled, shifted)

def merge_pair(first_schur, second_schur, first_rhs, second_rhs):
    middle = first_schur.shape[0] // 2
    coupled, shifted = eliminate(first_schur[middle:], second_schur[middle:], first_rhs[middle:] + second_rhs[middle:], middle)
    zero_block = jnp.zeros((middle, middle), jnp.float32)
    upper_rows = jnp.concatenate([first_schur[:middle, :middle], zero_block], axis=1) - jnp.dot(first_schur[:middle, middle:], coupled, precision=highest)
    lower_rows = jnp.concatenate([zero_block, second_schur[:middle, :middle]], axis=1) - jnp.dot(second_schur[:middle, middle:], coupled, precision=highest)
    upper_rhs = first_rhs[:middle] - jnp.dot(first_schur[:middle, middle:], shifted, precision=highest)
    lower_rhs = second_rhs[:middle] - jnp.dot(second_schur[:middle, middle:], shifted, precision=highest)
    parent = jnp.concatenate([upper_rows, lower_rows], axis=0)
    parent_rhs = jnp.concatenate([upper_rhs, lower_rhs])
    return (parent, parent_rhs, coupled, shifted)

def reference(adjoint_state, adjoint_source, reaction_rate, jacobian, lifting, separator, leaf_schur):
    residual = residual_field(adjoint_state, adjoint_source, reaction_rate, jacobian)
    residual_blocks = to_blocks(residual)
    lifting_blocks = to_blocks(lifting)
    picked = jnp.take_along_axis(residual_blocks, separator[:, :, :, None, :].astype(jnp.int32), axis=4)
    picked = jnp.swapaxes(picked, 3, 4)
    lifted = jnp.einsum('azbck,azbvk->azbcv', lifting_blocks, residual_blocks, precision=highest)
    width = SEP * NVAR
    middle = width // 2
    rhs = (picked + lifted).reshape(-1, width)
    schur = leaf_schur.reshape(-1, width, width)
    saved_levels = []
    while schur.shape[0] > 1:
        paired = schur.reshape(-1, 2, width, width)
        paired_rhs = rhs.reshape(-1, 2, width)
        schur, rhs, coupled, shifted = jax.vmap(merge_pair)(paired[:, 0], paired[:, 1], paired_rhs[:, 0], paired_rhs[:, 1])
        saved_levels.append((coupled, shifted))
    root_factor = jnp.linalg.cholesky(schur[0])
    inner = jax.scipy.linalg.solve_triangular(root_factor, rhs[0], lower=True)
    answer = jax.scipy.linalg.solve_triangular(root_factor, inner, lower=True, trans=1)[None, :]
    for coupled, shifted in reversed(saved_levels):
        separator_values = shifted - jnp.einsum('phw,pw->ph', coupled, answer, precision=highest)
        first_child = jnp.concatenate([answer[:, :middle], separator_values], axis=1)
        second_child = jnp.concatenate([answer[:, middle:], separator_values], axis=1)
        answer = jnp.stack([first_child, second_child], axis=1).reshape(-1, width)
    return answer.reshape(N_AXIAL, N_AZIM, N_BANK, width)
```

```python
import functools

import jax
import jax.numpy as jnp
from jax import lax
from jax.experimental import pallas as pl
from jax.experimental.pallas import tpu as pltpu
from jax.sharding import PartitionSpec as P

highest = lax.Precision.HIGHEST
everywhere = ("axial", "azim", "bank")
sub = 16
panel = 64
lanes = 128


def mm(a, b):
    return jnp.dot(a, b, precision=highest, preferred_element_type=jnp.float32)


def mm_nt(a, b):
    dims = (((1,), (1,)), ((), ()))
    return lax.dot_general(a, b, dims, precision=highest, preferred_element_type=jnp.float32)


def invert_small(cols):
    size, wide = cols[0].shape
    groups = size // 8
    rows = lax.broadcasted_iota(jnp.int32, (8, wide), 0)
    parts = [[c[8 * g : 8 * g + 8] for g in range(groups)] for c in cols]
    for k in range(size):
        home, row = divmod(k, 8)
        mask = rows == row
        pivot_col = parts[k]
        inverse = jnp.broadcast_to(1.0 / pivot_col[home][row : row + 1], (8, wide))
        scaled = [c * inverse for c in pivot_col]
        new = []
        for j in range(size):
            if j == k:
                new.append(
                    [jnp.where(mask, inverse, -scaled[g]) if g == home else -scaled[g] for g in range(groups)]
                )
                continue
            entry = jnp.broadcast_to(parts[j][home][row : row + 1], (8, wide))
            out = []
            for g in range(groups):
                if j == k + 1:
                    value = parts[j][g] - (pivot_col[g] * entry) * inverse
                else:
                    value = parts[j][g] - scaled[g] * entry
                if g == home:
                    value = jnp.where(mask, entry * inverse, value)
                out.append(value)
            new.append(out)
        parts = new
    return [jnp.concatenate(p, axis=0) for p in parts]


def sweep_panel(w, first):
    rows, n = w.shape
    lane = lax.broadcasted_iota(jnp.int32, (1, n), 1)
    row_of = lax.broadcasted_iota(jnp.int32, (sub, n), 0)
    wide = -(-n // lanes)

    def spread(c):
        return jnp.concatenate([c] * wide, axis=1)[:, :n]

    for s in range(rows // sub):
        lo = s * sub
        start = first + lo
        cols = [jnp.broadcast_to(w[:, start + j : start + j + 1], (rows, lanes)) for j in range(sub)]
        inverse = invert_small([c[lo : lo + sub] for c in cols])
        inside = (lane >= start) & (lane < start + sub)
        own = jnp.where(inside, jnp.where(row_of + start == lane, 1.0, 0.0), w[lo : lo + sub])
        solved = spread(inverse[0]) * own[0:1]
        for m in range(1, sub):
            solved = solved + spread(inverse[m]) * own[m : m + 1]
        pieces = []
        for q in range(rows // sub):
            if q == s:
                pieces.append(solved)
                continue
            value = jnp.where(inside, 0.0, w[q * sub : q * sub + sub])
            for m in range(sub):
                value = value - spread(cols[m][q * sub : q * sub + sub]) * solved[m : m + 1]
            pieces.append(value)
        w = jnp.concatenate(pieces, axis=0)
    return w


def invert(a):
    n = a.shape[0]
    lane = lax.broadcasted_iota(jnp.int32, (1, n), 1)
    for p in range(n // panel):
        lo = p * panel
        w = sweep_panel(a[lo : lo + panel], lo)
        inside = (lane >= lo) & (lane < lo + panel)
        new = []
        for q in range(n // panel):
            if q == p:
                new.append(w)
                continue
            old = a[q * panel : q * panel + panel]
            new.append(jnp.where(inside, 0.0, old) - mm(old[:, lo : lo + panel], w))
        a = jnp.concatenate(new, axis=0)
    return a


def pack_symmetric(m):
    third = m.shape[0] // 3
    top = m[:third, : 2 * third]
    mid = m[third : 2 * third, third:]
    low = jnp.concatenate([m[2 * third :, :third], m[2 * third :, 2 * third :]], axis=1)
    return jnp.concatenate([top, mid, low], axis=0)


def unpack_symmetric(p):
    third = p.shape[0] // 3
    top, mid, low = p[:third], p[third : 2 * third], p[2 * third :]
    rows = [
        jnp.concatenate([top, low[:, :third].T], axis=1),
        jnp.concatenate([top[:, third:].T, mid], axis=1),
        jnp.concatenate([low[:, :third], mid[:, third:].T, low[:, third:]], axis=1),
    ]
    return jnp.concatenate(rows, axis=0)


def pack_full(m):
    half = m.shape[0] // 2
    tail = jnp.concatenate([m[:half, lanes:], m[half:, lanes:]], axis=1)
    return jnp.concatenate([m[:, :lanes], tail], axis=0)


def unpack_full(p):
    n = p.shape[0] * 2 // 3
    tail = p[n:]
    rest = jnp.concatenate([tail[:, : lanes // 2], tail[:, lanes // 2 :]], axis=0)
    return jnp.concatenate([p[:n], rest], axis=1)


def to_row(f):
    return jnp.concatenate([f[i : i + 1] for i in range(3)], axis=1)


def from_row(row):
    parts = [row[:, i * lanes : (i + 1) * lanes] for i in range(3)]
    return jnp.concatenate(parts + [jnp.zeros((5, lanes), jnp.float32)], axis=0)


def leaf_kernel(sep_ref, state_ref, source_ref, rate_ref, jac_ref, lift_ref, before_ref, after_ref, left_ref, right_ref, f_ref):
    seps = sep_ref.shape[0]
    rows = rate_ref.shape[0]
    width = rate_ref.shape[1]
    chans = jac_ref.shape[0]
    c_of = lax.broadcasted_iota(jnp.int32, (8, width), 0)
    lane = lax.broadcasted_iota(jnp.int32, (8, width), 1)
    where = jnp.full((8, width), -1, jnp.int32)
    for c in range(seps):
        where = jnp.where(c_of == c, sep_ref[c], where)
    lift = []
    for i in range(rows):
        own = lift_ref[:, i, :]
        own = jnp.concatenate([own, jnp.zeros((8 - seps, width), jnp.float32)], axis=0)
        lift.append(own + jnp.where(where == lane + i * width, 1.0, 0.0))
    zero = jnp.zeros((8, width), jnp.float32)
    total = jnp.zeros((8, chans), jnp.float32)
    reacted = jnp.zeros((8, chans), jnp.float32)
    for i in range(rows):
        own = lift[i]
        around = (lift[i - 1] if i > 0 else zero) + (lift[i + 1] if i + 1 < rows else zero)
        around = around + jnp.where(lane == 0, 0.0, pltpu.roll(own, 1, 1))
        around = around + jnp.where(lane == width - 1, 0.0, pltpu.roll(own, width - 1, 1))
        both = jnp.concatenate([0.5 * around - 2.0 * own, own * rate_ref[i : i + 1, :]], axis=0)
        prod = mm_nt(both, state_ref[:, i, :])
        total = total + prod[:8] + mm_nt(own, source_ref[:, i, :])
        reacted = reacted + prod[8:]
    total = total - mm(reacted, jac_ref[...])
    edge = mm_nt(lift[0], before_ref[...]) + mm_nt(lift[-1], after_ref[...])
    first = jnp.concatenate([own[:, :1] for own in lift], axis=1)
    last = jnp.concatenate([own[:, width - 1 :] for own in lift], axis=1)
    edge = edge + mm_nt(first, left_ref[...]) + mm_nt(last, right_ref[...])
    total = total + 0.5 * edge
    out = [jnp.concatenate([total[2 * i : 2 * i + 1], total[2 * i + 1 : 2 * i + 2]], axis=1) for i in range(seps // 2)]
    out.append(jnp.zeros((8 - seps // 2, lanes), jnp.float32))
    f_ref[...] = jnp.concatenate(out, axis=0)


def order(upper, own, other):
    return jnp.where(upper, other, own), jnp.where(upper, own, other)


def first_kernel(upper_ref, own_ref, other_ref, ss_ref, rest_ref, xt_ref, inv_ref):
    half = own_ref.shape[0] // 2
    upper = upper_ref[0] != 0
    inverse = invert(own_ref[half:, half:] + other_ref[half:, half:])
    inv_ref[...] = inverse
    os1, os2 = order(upper, own_ref[:half, half:], other_ref[:half, half:])
    oo1, oo2 = order(upper, own_ref[:half, :half], other_ref[:half, :half])
    xt = mm(jnp.concatenate([os1, os2], axis=0), inverse)
    xt_ref[...] = xt
    ss_ref[...] = pack_symmetric(oo2 - mm_nt(xt[half:], os2))
    rest_ref[:half, :] = pack_symmetric(oo1 - mm_nt(xt[:half], os1))
    rest_ref[half:, :] = pack_full(-mm_nt(xt[:half], os2))


def first_rhs_kernel(upper_ref, own_ref, other_ref, inv_ref, xt_ref, z_ref, f_ref):
    half = inv_ref.shape[0]
    upper = upper_ref[0] != 0
    own, other = to_row(own_ref[...]), to_row(other_ref[...])
    first, second = order(upper, own, other)
    shared = own[:, half:] + other[:, half:]
    z_ref[...] = mm(shared, inv_ref[...])
    outer = jnp.concatenate([first[:, :half], second[:, :half]], axis=1)
    f_ref[...] = from_row(outer - mm_nt(shared, xt_ref[...]))


def factor_kernel(own_ref, other_ref, inv_ref):
    inv_ref[...] = invert(unpack_symmetric(own_ref[...] + other_ref[...]))


def merged(upper_ref, inv_ref, own_ref, other_ref, own_f, other_f):
    half = inv_ref.shape[0]
    upper = upper_ref[0] != 0
    full = half * 3 // 2
    oo1, oo2 = order(upper, own_ref[:half, :], other_ref[:half, :])
    os1, os2 = order(upper, own_ref[half : half + full, :], other_ref[half : half + full, :])
    os1, os2 = unpack_full(os1), unpack_full(os2)
    own, other = to_row(own_f), to_row(other_f)
    first, second = order(upper, own, other)
    shared = own[:, half:] + other[:, half:]
    outer = jnp.concatenate([first[:, :half], second[:, :half]], axis=1)
    stacked = jnp.concatenate([os1, os2, jnp.broadcast_to(shared, (8, half))], axis=0)
    xt = mm(stacked, inv_ref[...])
    z = xt[2 * half : 2 * half + 1]
    ss = unpack_symmetric(oo2) - mm_nt(xt[half : 2 * half], os2)
    oo = unpack_symmetric(oo1) - mm_nt(xt[:half], os1)
    cross = -mm_nt(xt[:half], os2)
    f = outer - jnp.concatenate([mm_nt(z, os1), mm_nt(z, os2)], axis=1)
    return xt[: 2 * half], z, oo, cross, ss, f


def update_kernel(upper_ref, inv_ref, own_ref, other_ref, own_f_ref, other_f_ref, ss_ref, rest_ref, xt_ref, z_ref):
    half = inv_ref.shape[0]
    full = half * 3 // 2
    xt, z, oo, cross, ss, f = merged(upper_ref, inv_ref, own_ref, other_ref, own_f_ref[...], other_f_ref[...])
    ss_ref[...] = pack_symmetric(ss)
    rest_ref[:half, :] = pack_symmetric(oo)
    rest_ref[half : half + full, :] = pack_full(cross)
    rest_ref[half + full :, :] = from_row(f)
    xt_ref[...] = xt
    z_ref[...] = z


def end_kernel(upper_ref, inv_ref, own_ref, other_ref, own_f_ref, other_f_ref, t_ref, xt_ref, z_ref, yt_ref, w_ref):
    half = inv_ref.shape[0]
    xt, z, oo, cross, ss, f = merged(upper_ref, inv_ref, own_ref, other_ref, own_f_ref[...], other_f_ref[...])
    xt_ref[...] = xt
    z_ref[...] = z
    inverse = invert(oo)
    stacked = jnp.concatenate([cross.T, jnp.broadcast_to(f[:, :half], (8, half))], axis=0)
    yt = mm(stacked, inverse)
    w = yt[half : half + 1]
    yt_ref[...] = yt[:half]
    w_ref[...] = w
    t_ref[:half, :] = pack_symmetric(ss - mm(yt[:half], cross))
    rest = jnp.concatenate([f[:, half:] - mm(w, cross), jnp.zeros((1, half), jnp.float32)], axis=1)
    t_ref[half:, :] = from_row(rest)


def solve_kernel(levels, uppers_ref, own_ref, other_ref, yt_ref, w_ref, *refs):
    half = yt_ref.shape[0]
    out_ref = refs[-1]
    total = own_ref[...] + other_ref[...]
    inverse = invert(unpack_symmetric(total[:half]))
    shared = mm(to_row(total[half:])[:, :half], inverse)
    answer = jnp.concatenate([w_ref[...] - mm(shared, yt_ref[...]), shared], axis=1)
    for level in reversed(range(levels)):
        inner = refs[2 * level + 1][...] - mm(answer, refs[2 * level][...])
        outer = jnp.where(uppers_ref[level] != 0, answer[:, half:], answer[:, :half])
        answer = jnp.concatenate([outer, inner], axis=1)
    out_ref[...] = answer


smem = pl.BlockSpec(memory_space=pltpu.SMEM)
vmem = pl.BlockSpec(memory_space=pltpu.VMEM)


def call(kernel, name, shapes, *operands, scalars=1):
    outs = tuple(jax.ShapeDtypeStruct(s, jnp.float32) for s in shapes)
    single = len(outs) == 1
    return pl.pallas_call(
        kernel,
        out_shape=outs[0] if single else outs,
        in_specs=[smem] * scalars + [vmem] * (len(operands) - scalars),
        out_specs=vmem if single else tuple(vmem for _ in outs),
        compiler_params=pltpu.CompilerParams(vmem_limit_bytes=32 << 20),
        name=name,
    )(*operands)


def partner(array, level):
    count = lax.axis_size(everywhere)
    return lax.ppermute(array, everywhere, [(i, i ^ 1 << level) for i in range(count)])


def halos(state):
    axial, azim = lax.axis_size("axial"), lax.axis_size("azim")
    up = [(i, i + 1) for i in range(axial - 1)]
    before = lax.ppermute(state[:, -1, :], "axial", up)
    after = lax.ppermute(state[:, 0, :], "axial", [(j, i) for i, j in up])
    around = [(i, (i + 1) % azim) for i in range(azim)]
    left = lax.ppermute(state[:, :, -1], "azim", around)
    right = lax.ppermute(state[:, :, 0], "azim", [(j, i) for i, j in around])
    return before, after, left, right


def body(adjoint_state, adjoint_source, reaction_rate, jacobian, lifting, separator, leaf_schur):
    chans, rows, cells = adjoint_state.shape[1:]
    width = leaf_schur.shape[-1]
    half = width // 2
    full = half * 3 // 2
    levels = lax.axis_size(everywhere).bit_length() - 1
    flat_index = lax.axis_index(everywhere)
    uppers = jnp.bitwise_and(jnp.right_shift(flat_index, jnp.arange(levels, dtype=jnp.int32)), 1)
    upper = [uppers[i : i + 1] for i in range(levels)]

    schur = leaf_schur.reshape(width, width)
    other_schur = partner(schur, 0)
    state = adjoint_state.reshape(chans, rows, cells)
    edges = halos(state)
    ss, rest, xt, inverse = call(
        first_kernel,
        "merge_leaves",
        [(half, lanes), (half + full, lanes), (width, half), (half, half)],
        upper[0],
        schur,
        other_schur,
    )
    other_ss = partner(ss, 1)
    other_rest = partner(rest, 1)
    f = call(
        leaf_kernel,
        "leaf_rhs",
        [(8, lanes)],
        separator.reshape(-1),
        state,
        adjoint_source.reshape(chans, rows, cells),
        reaction_rate.reshape(rows, cells),
        jacobian.reshape(chans, chans),
        lifting.reshape(-1, rows, cells),
        *edges,
    )
    z, f = call(first_rhs_kernel, "merge_leaf_rhs", [(1, half), (8, lanes)], upper[0], f, partner(f, 0), inverse, xt)
    other_f = partner(f, 1)
    saved = [xt, z]
    for level in range(1, levels - 1):
        inverse = call(factor_kernel, f"factor_{level}", [(half, half)], ss, other_ss, scalars=0)
        operands = (upper[level], inverse, rest, other_rest, f, other_f)
        if level < levels - 2:
            ss, rest, xt, z = call(
                update_kernel,
                f"update_{level}",
                [(half, lanes), (half + full + 8, lanes), (width, half), (1, half)],
                *operands,
            )
            other_ss = partner(ss, level + 1)
            other_rest = partner(rest, level + 1)
            f, other_f = rest[half + full :], other_rest[half + full :]
        else:
            end, xt, z, yt, w = call(
                end_kernel,
                f"update_{level}",
                [(half + 8, lanes), (width, half), (1, half), (half, half), (1, half)],
                *operands,
            )
        saved += [xt, z]
    answer = call(
        functools.partial(solve_kernel, levels - 1),
        "solve",
        [(1, width)],
        uppers,
        end,
        partner(end, levels - 1),
        yt,
        w,
        *saved,
    )
    return answer.reshape(1, 1, 1, width)


def solution(mesh):
    in_specs = (
        P("bank", None, "axial", "azim"),
        P("bank", None, "axial", "azim"),
        P("bank", "axial", "azim"),
        P("bank", None, None),
        P("bank", None, "axial", "azim"),
        P("axial", "azim", "bank", None),
        P("axial", "azim", "bank", None, None),
    )
    out_specs = P("axial", "azim", "bank", None)
    return jax.shard_map(body, mesh=mesh, in_specs=in_specs, out_specs=out_specs, check_vma=False)
```

```python
import functools

import jax
import jax.numpy as jnp
from jax import lax
from jax.experimental import pallas as pl
from jax.experimental.pallas import tpu as pltpu
from jax.sharding import PartitionSpec as P

highest = lax.Precision.HIGHEST
everywhere = ("axial", "azim", "bank")
sub = 16
panel = 64
lanes = 128


def mm(a, b):
    return jnp.dot(a, b, precision=highest, preferred_element_type=jnp.float32)


def mm_nt(a, b):
    dims = (((1,), (1,)), ((), ()))
    return lax.dot_general(a, b, dims, precision=highest, preferred_element_type=jnp.float32)


def invert_small(cols):
    size, wide = cols[0].shape
    groups = size // 8
    rows = lax.broadcasted_iota(jnp.int32, (8, wide), 0)
    parts = [[c[8 * g : 8 * g + 8] for g in range(groups)] for c in cols]
    for k in range(size):
        home, row = divmod(k, 8)
        mask = rows == row
        pivot_col = parts[k]
        inverse = jnp.broadcast_to(1.0 / pivot_col[home][row : row + 1], (8, wide))
        scaled = [c * inverse for c in pivot_col]
        new = []
        for j in range(size):
            if j == k:
                new.append(
                    [jnp.where(mask, inverse, -scaled[g]) if g == home else -scaled[g] for g in range(groups)]
                )
                continue
            entry = jnp.broadcast_to(parts[j][home][row : row + 1], (8, wide))
            out = []
            for g in range(groups):
                if j == k + 1:
                    value = parts[j][g] - (pivot_col[g] * entry) * inverse
                else:
                    value = parts[j][g] - scaled[g] * entry
                if g == home:
                    value = jnp.where(mask, entry * inverse, value)
                out.append(value)
            new.append(out)
        parts = new
    return [jnp.concatenate(p, axis=0) for p in parts]


def sweep_panel(w, first):
    rows, n = w.shape
    lane = lax.broadcasted_iota(jnp.int32, (1, n), 1)
    row_of = lax.broadcasted_iota(jnp.int32, (sub, n), 0)
    wide = -(-n // lanes)

    def spread(c):
        return jnp.concatenate([c] * wide, axis=1)[:, :n]

    for s in range(rows // sub):
        lo = s * sub
        start = first + lo
        cols = [jnp.broadcast_to(w[:, start + j : start + j + 1], (rows, lanes)) for j in range(sub)]
        inverse = invert_small([c[lo : lo + sub] for c in cols])
        inside = (lane >= start) & (lane < start + sub)
        own = jnp.where(inside, jnp.where(row_of + start == lane, 1.0, 0.0), w[lo : lo + sub])
        solved = spread(inverse[0]) * own[0:1]
        for m in range(1, sub):
            solved = solved + spread(inverse[m]) * own[m : m + 1]
        pieces = []
        for q in range(rows // sub):
            if q == s:
                pieces.append(solved)
                continue
            value = jnp.where(inside, 0.0, w[q * sub : q * sub + sub])
            for m in range(sub):
                value = value - spread(cols[m][q * sub : q * sub + sub]) * solved[m : m + 1]
            pieces.append(value)
        w = jnp.concatenate(pieces, axis=0)
    return w


def invert(a):
    n = a.shape[0]
    lane = lax.broadcasted_iota(jnp.int32, (1, n), 1)
    for p in range(n // panel):
        lo = p * panel
        w = sweep_panel(a[lo : lo + panel], lo)
        inside = (lane >= lo) & (lane < lo + panel)
        new = []
        for q in range(n // panel):
            if q == p:
                new.append(w)
                continue
            old = a[q * panel : q * panel + panel]
            new.append(jnp.where(inside, 0.0, old) - mm(old[:, lo : lo + panel], w))
        a = jnp.concatenate(new, axis=0)
    return a


def pack_symmetric(m):
    third = m.shape[0] // 3
    top = m[:third, : 2 * third]
    mid = m[third : 2 * third, third:]
    low = jnp.concatenate([m[2 * third :, :third], m[2 * third :, 2 * third :]], axis=1)
    return jnp.concatenate([top, mid, low], axis=0)


def unpack_symmetric(p):
    third = p.shape[0] // 3
    top, mid, low = p[:third], p[third : 2 * third], p[2 * third :]
    rows = [
        jnp.concatenate([top, low[:, :third].T], axis=1),
        jnp.concatenate([top[:, third:].T, mid], axis=1),
        jnp.concatenate([low[:, :third], mid[:, third:].T, low[:, third:]], axis=1),
    ]
    return jnp.concatenate(rows, axis=0)


def pack_full(m):
    half = m.shape[0] // 2
    tail = jnp.concatenate([m[:half, lanes:], m[half:, lanes:]], axis=1)
    return jnp.concatenate([m[:, :lanes], tail], axis=0)


def unpack_full(p):
    n = p.shape[0] * 2 // 3
    tail = p[n:]
    rest = jnp.concatenate([tail[:, : lanes // 2], tail[:, lanes // 2 :]], axis=0)
    return jnp.concatenate([p[:n], rest], axis=1)


def to_row(f):
    return jnp.concatenate([f[i : i + 1] for i in range(3)], axis=1)


def from_row(row):
    parts = [row[:, i * lanes : (i + 1) * lanes] for i in range(3)]
    return jnp.concatenate(parts + [jnp.zeros((5, lanes), jnp.float32)], axis=0)


def leaf_kernel(sep_ref, after_this_ref, state_ref, source_ref, rate_ref, jac_ref, lift_ref, before_ref, after_ref, left_ref, right_ref, f_ref):
    seps = sep_ref.shape[0]
    rows = rate_ref.shape[0]
    width = rate_ref.shape[1]
    chans = jac_ref.shape[0]
    c_of = lax.broadcasted_iota(jnp.int32, (8, width), 0)
    lane = lax.broadcasted_iota(jnp.int32, (8, width), 1)
    where = jnp.full((8, width), -1, jnp.int32)
    for c in range(seps):
        where = jnp.where(c_of == c, sep_ref[c], where)
    lift = []
    for i in range(rows):
        own = lift_ref[:, i, :]
        own = jnp.concatenate([own, jnp.zeros((8 - seps, width), jnp.float32)], axis=0)
        lift.append(own + jnp.where(where == lane + i * width, 1.0, 0.0))
    zero = jnp.zeros((8, width), jnp.float32)
    total = jnp.zeros((8, chans), jnp.float32)
    reacted = jnp.zeros((8, chans), jnp.float32)
    for i in range(rows):
        own = lift[i]
        around = (lift[i - 1] if i > 0 else zero) + (lift[i + 1] if i + 1 < rows else zero)
        around = around + jnp.where(lane == 0, 0.0, pltpu.roll(own, 1, 1))
        around = around + jnp.where(lane == width - 1, 0.0, pltpu.roll(own, width - 1, 1))
        both = jnp.concatenate([0.5 * around - 2.0 * own, own * rate_ref[i : i + 1, :]], axis=0)
        prod = mm_nt(both, state_ref[:, i, :])
        total = total + prod[:8] + mm_nt(own, source_ref[:, i, :])
        reacted = reacted + prod[8:]
    total = total - mm(reacted, jac_ref[...])
    edge = mm_nt(lift[0], before_ref[...]) + mm_nt(lift[-1], after_ref[...])
    first = jnp.concatenate([own[:, :1] for own in lift], axis=1)
    last = jnp.concatenate([own[:, width - 1 :] for own in lift], axis=1)
    edge = edge + mm_nt(first, left_ref[...]) + mm_nt(last, right_ref[...])
    total = total + 0.5 * edge
    out = [jnp.concatenate([total[2 * i : 2 * i + 1], total[2 * i + 1 : 2 * i + 2]], axis=1) for i in range(seps // 2)]
    out.append(jnp.zeros((8 - seps // 2, lanes), jnp.float32))
    f_ref[...] = jnp.concatenate(out, axis=0)


def edges_kernel(state_ref, top_ref, bottom_ref, sides_ref):
    chans, rows, cells = state_ref.shape
    top_ref[...] = state_ref[:, 0, :]
    bottom_ref[...] = state_ref[:, rows - 1, :]
    left = jnp.concatenate([state_ref[:, i, :1] for i in range(rows)], axis=1)
    right = jnp.concatenate([state_ref[:, i, cells - 1 :] for i in range(rows)], axis=1)
    sides_ref[...] = jnp.concatenate([left, right], axis=0)


def order(upper, own, other):
    return jnp.where(upper, other, own), jnp.where(upper, own, other)


def first_kernel(upper_ref, own_ref, other_ref, ss_ref, inv_ref, xt_ref):
    half = own_ref.shape[0] // 2
    upper = upper_ref[0] != 0
    inverse = invert(own_ref[half:, half:] + other_ref[half:, half:])
    inv_ref[...] = inverse
    _, os2 = order(upper, own_ref[:half, half:], other_ref[:half, half:])
    _, oo2 = order(upper, own_ref[:half, :half], other_ref[:half, :half])
    xt2 = mm(os2, inverse)
    xt_ref[...] = xt2
    ss_ref[...] = pack_symmetric(oo2 - mm_nt(xt2, os2))


def factor_kernel(own_ref, other_ref, inv_ref):
    inv_ref[...] = invert(unpack_symmetric(own_ref[...] + other_ref[...]))


def shared_kernel(upper_ref, inv_ref, own_ref, other_ref, ss_ref, xt_ref):
    half = inv_ref.shape[0]
    full = half * 3 // 2
    upper = upper_ref[0] != 0
    _, oo2 = order(upper, own_ref[:half, :], other_ref[:half, :])
    _, os2 = order(upper, own_ref[half : half + full, :], other_ref[half : half + full, :])
    os2 = unpack_full(os2)
    xt2 = mm(os2, inv_ref[...])
    xt_ref[...] = xt2
    ss_ref[...] = pack_symmetric(unpack_symmetric(oo2) - mm_nt(xt2, os2))


def merge(upper, inverse, xt2, os1, os2, oo1, own_f, other_f):
    half = inverse.shape[0]
    own, other = to_row(own_f), to_row(other_f)
    first, second = order(upper, own, other)
    shared = own[:, half:] + other[:, half:]
    outer = jnp.concatenate([first[:, :half], second[:, :half]], axis=1)
    xt = mm(jnp.concatenate([os1, jnp.broadcast_to(shared, (8, half))], axis=0), inverse)
    z = xt[half : half + 1]
    both = mm_nt(xt, jnp.concatenate([os1, os2], axis=0))
    oo = oo1 - both[:half, :half]
    cross = -both[:half, half:]
    f = outer - both[half : half + 1]
    return jnp.concatenate([xt[:half], xt2], axis=0), z, oo, cross, f


def put_rest(rest_ref, oo, cross, f):
    half = oo.shape[0]
    full = half * 3 // 2
    rest_ref[:half, :] = pack_symmetric(oo)
    rest_ref[half : half + full, :] = pack_full(cross)
    rest_ref[half + full :, :] = from_row(f)


def first_rest_kernel(upper_ref, inv_ref, xt2_ref, own_ref, other_ref, own_f_ref, other_f_ref, rest_ref, xt_ref, z_ref):
    half = inv_ref.shape[0]
    upper = upper_ref[0] != 0
    os1, os2 = order(upper, own_ref[:half, half:], other_ref[:half, half:])
    oo1, _ = order(upper, own_ref[:half, :half], other_ref[:half, :half])
    xt_ref[...], z_ref[...], oo, cross, f = merge(upper, inv_ref[...], xt2_ref[...], os1, os2, oo1, own_f_ref[...], other_f_ref[...])
    put_rest(rest_ref, oo, cross, f)


def unpacked(upper, own_ref, other_ref, half):
    full = half * 3 // 2
    oo1, oo2 = order(upper, own_ref[:half, :], other_ref[:half, :])
    os1, os2 = order(upper, own_ref[half : half + full, :], other_ref[half : half + full, :])
    return unpack_full(os1), unpack_full(os2), oo1, oo2, own_ref[half + full :, :], other_ref[half + full :, :]


def rest_kernel(upper_ref, inv_ref, xt2_ref, own_ref, other_ref, rest_ref, xt_ref, z_ref):
    upper = upper_ref[0] != 0
    os1, os2, oo1, _, own_f, other_f = unpacked(upper, own_ref, other_ref, inv_ref.shape[0])
    oo1 = unpack_symmetric(oo1)
    xt_ref[...], z_ref[...], oo, cross, f = merge(upper, inv_ref[...], xt2_ref[...], os1, os2, oo1, own_f, other_f)
    put_rest(rest_ref, oo, cross, f)


def end_kernel(upper_ref, inv_ref, own_ref, other_ref, t_ref, xt_ref, z_ref, yt_ref, w_ref):
    half = inv_ref.shape[0]
    upper = upper_ref[0] != 0
    os1, os2, oo1, oo2, own_f, other_f = unpacked(upper, own_ref, other_ref, half)
    oo1 = unpack_symmetric(oo1)
    xt2 = mm(os2, inv_ref[...])
    xt, z, oo, cross, f = merge(upper, inv_ref[...], xt2, os1, os2, oo1, own_f, other_f)
    ss = unpack_symmetric(oo2) - mm_nt(xt[half:], os2)
    xt_ref[...] = xt
    z_ref[...] = z
    inverse = invert(oo)
    stacked = jnp.concatenate([cross.T, jnp.broadcast_to(f[:, :half], (8, half))], axis=0)
    yt = mm(stacked, inverse)
    w = yt[half : half + 1]
    yt_ref[...] = yt[:half]
    w_ref[...] = w
    t_ref[:half, :] = pack_symmetric(ss - mm(yt[:half], cross))
    rest = jnp.concatenate([f[:, half:] - mm(w, cross), jnp.zeros((1, half), jnp.float32)], axis=1)
    t_ref[half:, :] = from_row(rest)


def compose_kernel(levels, uppers_ref, yt_ref, w_ref, *refs):
    half = yt_ref.shape[0]
    out_ref = refs[-1]
    row = lax.broadcasted_iota(jnp.int32, (half + 8, half), 0)
    col = lax.broadcasted_iota(jnp.int32, (half + 8, half), 1)
    outer = jnp.concatenate([-yt_ref[...], jnp.broadcast_to(w_ref[...], (8, half))], axis=0)
    answer = jnp.concatenate([outer, jnp.where(row == col, 1.0, 0.0)], axis=1)
    for level in reversed(range(levels)):
        inner = jnp.where(row >= half, refs[2 * level + 1][...], 0.0) - mm(answer, refs[2 * level][...])
        outer = jnp.where(uppers_ref[level] != 0, answer[:, half:], answer[:, :half])
        answer = jnp.concatenate([outer, inner], axis=1)
    out_ref[...] = answer


def solve_kernel(own_ref, other_ref, map_ref, out_ref):
    half = map_ref.shape[0] - 8
    total = own_ref[...] + other_ref[...]
    inverse = invert(unpack_symmetric(total[:half]))
    shared = mm(to_row(total[half:])[:, :half], inverse)
    out_ref[...] = mm(shared, map_ref[:half, :]) + map_ref[half : half + 1, :]


smem = pl.BlockSpec(memory_space=pltpu.SMEM)
vmem = pl.BlockSpec(memory_space=pltpu.VMEM)


def call(kernel, name, shapes, micros, *operands, scalars=1):
    outs = tuple(jax.ShapeDtypeStruct(s, jnp.float32) for s in shapes)
    single = len(outs) == 1
    return pl.pallas_call(
        kernel,
        out_shape=outs[0] if single else outs,
        in_specs=[smem] * scalars + [vmem] * (len(operands) - scalars),
        out_specs=vmem if single else tuple(vmem for _ in outs),
        compiler_params=pltpu.CompilerParams(vmem_limit_bytes=32 << 20),
        cost_estimate=pl.CostEstimate(flops=int(micros * 1e9), bytes_accessed=0, transcendentals=0),
        name=name,
    )(*operands)


def partner(array, level):
    count = lax.axis_size(everywhere)
    return lax.ppermute(array, everywhere, [(i, i ^ 1 << level) for i in range(count)])


def halos(state):
    chans, rows, cells = state.shape
    axial, azim = lax.axis_size("axial"), lax.axis_size("azim")
    top, bottom, sides = call(
        edges_kernel, "edges", [(chans, cells), (chans, cells), (2 * chans, rows)], 0.5, state, scalars=0
    )
    up = [(i, i + 1) for i in range(axial - 1)]
    before = lax.ppermute(bottom, "axial", up)
    after = lax.ppermute(top, "axial", [(j, i) for i, j in up])
    around = [(i, (i + 1) % azim) for i in range(azim)]
    if azim == 2:
        sides = lax.ppermute(sides, "azim", around)
        left, right = sides[chans:], sides[:chans]
    else:
        left = lax.ppermute(sides[chans:], "azim", around)
        right = lax.ppermute(sides[:chans], "azim", [(j, i) for i, j in around])
    return before, after, left, right


def body(adjoint_state, adjoint_source, reaction_rate, jacobian, lifting, separator, leaf_schur):
    chans, rows, cells = adjoint_state.shape[1:]
    width = leaf_schur.shape[-1]
    half = width // 2
    full = half * 3 // 2
    levels = lax.axis_size(everywhere).bit_length() - 1
    flat_index = lax.axis_index(everywhere)
    uppers = jnp.bitwise_and(jnp.right_shift(flat_index, jnp.arange(levels, dtype=jnp.int32)), 1)
    upper = [uppers[i : i + 1] for i in range(levels)]
    rest_shapes = [(half + full + 8, lanes), (width, half), (1, half)]

    schur = leaf_schur.reshape(width, width)
    other_schur = partner(schur, 0)
    state = adjoint_state.reshape(chans, rows, cells)
    edges = halos(state)
    ss, inverse, xt2 = call(
        first_kernel, "factor_0", [(half, lanes), (half, half), (half, half)], 8.0, upper[0], schur, other_schur
    )
    other_ss = partner(ss, 1)
    f = call(
        leaf_kernel,
        "leaf_rhs",
        [(8, lanes)],
        2.3,
        separator.reshape(-1),
        ss,
        state,
        adjoint_source.reshape(chans, rows, cells),
        reaction_rate.reshape(rows, cells),
        jacobian.reshape(chans, chans),
        lifting.reshape(-1, rows, cells),
        *edges,
    )
    rest, xt, z = call(
        first_rest_kernel, "rest_0", rest_shapes, 1.7, upper[0], inverse, xt2, schur, other_schur, f, partner(f, 0)
    )
    other_rest = partner(rest, 1)
    saved = [xt, z]
    for level in range(1, levels - 1):
        inverse = call(factor_kernel, f"factor_{level}", [(half, half)], 6.5, ss, other_ss, scalars=0)
        if level < levels - 2:
            ss, xt2 = call(
                shared_kernel,
                f"shared_{level}",
                [(half, lanes), (half, half)],
                1.5,
                upper[level],
                inverse,
                rest,
                other_rest,
            )
            other_ss = partner(ss, level + 1)
            rest, xt, z = call(
                rest_kernel, f"rest_{level}", rest_shapes, 1.7, upper[level], inverse, xt2, rest, other_rest
            )
            other_rest = partner(rest, level + 1)
        else:
            end, xt, z, yt, w = call(
                end_kernel,
                f"end_{level}",
                [(half + 8, lanes), (width, half), (1, half), (half, half), (1, half)],
                9.5,
                upper[level],
                inverse,
                rest,
                other_rest,
            )
        saved += [xt, z]
    other_end = partner(end, levels - 1)
    composed = call(
        functools.partial(compose_kernel, levels - 1), "compose", [(half + 8, width)], 3.7, uppers, yt, w, *saved
    )
    answer = call(solve_kernel, "solve", [(1, width)], 7.0, end, other_end, composed, scalars=0)
    return answer.reshape(1, 1, 1, width)


def solution(mesh):
    in_specs = (
        P("bank", None, "axial", "azim"),
        P("bank", None, "axial", "azim"),
        P("bank", "axial", "azim"),
        P("bank", None, None),
        P("bank", None, "axial", "azim"),
        P("axial", "azim", "bank", None),
        P("axial", "azim", "bank", None, None),
    )
    out_specs = P("axial", "azim", "bank", None)
    return jax.shard_map(body, mesh=mesh, in_specs=in_specs, out_specs=out_specs, check_vma=False)
```

```python
import functools

import jax
import jax.numpy as jnp
from jax import lax
from jax.experimental import pallas as pl
from jax.experimental.pallas import tpu as pltpu
from jax.sharding import PartitionSpec as P

highest = lax.Precision.HIGHEST
everywhere = ("axial", "azim", "bank")
panel = 64
lanes = 128


def mm(a, b):
    return jnp.dot(a, b, precision=highest, preferred_element_type=jnp.float32)


def mm_nt(a, b):
    dims = (((1,), (1,)), ((), ()))
    return lax.dot_general(a, b, dims, precision=highest, preferred_element_type=jnp.float32)


def sweep_panel(groups, first):
    n = len(groups)
    groups = [list(g) for g in groups]
    widths = [t.shape[1] for t in groups[0]]
    row = lax.broadcasted_iota(jnp.int32, (8, lanes), 0)
    lane_of = [lax.broadcasted_iota(jnp.int32, (8, w), 1) for w in widths]
    row_of = [lax.broadcasted_iota(jnp.int32, (8, w), 0) for w in widths]

    def columns(q, s):
        tile, lane = divmod(first + 8 * s, lanes)
        return [jnp.broadcast_to(groups[q][tile][:, lane + m : lane + m + 1], (8, lanes)) for m in range(8)]

    def across(column, tile):
        return column if widths[tile] == lanes else column[:, : widths[tile]]

    def spread(value, i):
        return jnp.broadcast_to(value[i : i + 1], value.shape)

    def inside(s):
        tile, lane = divmod(first + 8 * s, lanes)
        return tile, lane, (lane_of[tile] >= lane) & (lane_of[tile] < lane + 8)

    def update(q, s, cols, solved):
        home, _, here = inside(s)
        new = []
        for k, tile in enumerate(groups[q]):
            value = jnp.where(here, 0.0, tile) if k == home else tile
            for m in range(8):
                value = value - across(cols[m], k) * spread(solved[k], m)
            new.append(value)
        groups[q] = new

    diag = columns(0, 0)
    cols = {q: columns(q, 0) for q in range(1, n)}
    pending = []
    for s in range(n):
        more = s + 1 < n
        if more:
            low, after = list(cols[s + 1]), columns(s + 1, s + 1)
        home, lane, here = inside(s)
        own = list(groups[s])
        own[home] = jnp.where(here, jnp.where(lane_of[home] - lane == row_of[home], 1.0, 0.0), own[home])
        scale = None
        for p in range(8):
            inverse = 1.0 / spread(diag[p], p)
            scale = inverse if scale is None else jnp.where(row == p, inverse, scale)
            factor = jnp.where(row == p, 0.0, diag[p] * inverse)
            if more:
                low_factor = low[p] * inverse
            for j in range(p + 1, 8):
                entry = spread(diag[j], p)
                diag[j] = diag[j] - factor * entry
                if more:
                    low[j] = low[j] - low_factor * entry
            if more:
                for j in range(8):
                    after[j] = after[j] - low_factor * spread(low[p], j)
            for k in range(len(own)):
                own[k] = own[k] - across(factor, k) * spread(own[k], p)
            if pending:
                q, *rest = pending.pop(0)
                update(q, *rest)
                cols[q] = columns(q, s)
        solved = [tile * across(scale, k) for k, tile in enumerate(own)]
        groups[s] = solved
        for q in list(range(s + 1, n)) + list(range(s)):
            if s < q < s + 3:
                update(q, s, cols[q], solved)
            else:
                pending.append((q, s, cols[q], solved))
        if more:
            diag = after
            cols[s] = columns(s, s + 1)
            if s + 2 < n:
                cols[s + 2] = columns(s + 2, s + 1)
    for work in pending:
        update(*work)
    return groups


def invert(slabs):
    slabs = list(slabs)
    n = len(slabs) * panel
    lane = lax.broadcasted_iota(jnp.int32, (1, n), 1)
    for p in range(len(slabs)):
        lo = p * panel
        w = slabs[p]
        groups = [[w[i : i + 8, t : min(t + lanes, n)] for t in range(0, n, lanes)] for i in range(0, panel, 8)]
        groups = sweep_panel(groups, lo)
        w = jnp.concatenate([jnp.concatenate(g, axis=1) for g in groups], axis=0)
        slabs[p] = w
        here = (lane >= lo) & (lane < lo + panel)
        for q in list(range(p + 1, len(slabs))) + list(range(p)):
            slabs[q] = jnp.where(here, 0.0, slabs[q]) - mm(slabs[q][:, lo : lo + panel], w)
    return jnp.concatenate(slabs, axis=0)


def invert_whole(a):
    return invert([a[i : i + panel] for i in range(0, a.shape[0], panel)])


def pack_symmetric(m):
    third = m.shape[0] // 3
    low = jnp.concatenate([m[:third, 2 * third :], m[2 * third :, 2 * third :]], axis=1)
    return jnp.concatenate([m[:third, : 2 * third], m[third : 2 * third, third:], low], axis=0)


def unpack_symmetric(p):
    third = p.shape[0] // 3
    top, mid, low = p[:third], p[third : 2 * third], p[2 * third :]
    return [
        jnp.concatenate([top, low[:, :third]], axis=1),
        jnp.concatenate([top[:, third:].T, mid], axis=1),
        jnp.concatenate([low[:, :third].T, mid[:, third:].T, low[:, third:]], axis=1),
    ]


def pack_full(m):
    half = m.shape[0] // 2
    tail = jnp.concatenate([m[:half, lanes:], m[half:, lanes:]], axis=1)
    return jnp.concatenate([m[:, :lanes], tail], axis=0)


def unpack_full(p):
    n = p.shape[0] * 2 // 3
    tail = p[n:]
    rest = jnp.concatenate([tail[:, : lanes // 2], tail[:, lanes // 2 :]], axis=0)
    return jnp.concatenate([p[:n], rest], axis=1)


def to_row(f):
    return jnp.concatenate([f[i : i + 1] for i in range(3)], axis=1)


def from_row(row):
    parts = [row[:, i * lanes : (i + 1) * lanes] for i in range(3)]
    return jnp.concatenate(parts + [jnp.zeros((5, lanes), jnp.float32)], axis=0)


def leaf_kernel(sep_ref, after_this_ref, state_ref, source_ref, rate_ref, jac_ref, lift_ref, before_ref, after_ref, sides_ref, f_ref):
    seps = sep_ref.shape[0]
    rows = rate_ref.shape[0]
    width = rate_ref.shape[1]
    chans = jac_ref.shape[0]
    c_of = lax.broadcasted_iota(jnp.int32, (8, width), 0)
    lane = lax.broadcasted_iota(jnp.int32, (8, width), 1)
    where = jnp.full((8, width), -1, jnp.int32)
    for c in range(seps):
        where = jnp.where(c_of == c, sep_ref[c], where)
    lift = []
    for i in range(rows):
        own = lift_ref[:, i, :]
        own = jnp.concatenate([own, jnp.zeros((8 - seps, width), jnp.float32)], axis=0)
        lift.append(own + jnp.where(where == lane + i * width, 1.0, 0.0))
    zero = jnp.zeros((8, width), jnp.float32)
    total = jnp.zeros((8, chans), jnp.float32)
    reacted = jnp.zeros((8, chans), jnp.float32)
    for i in range(rows):
        own = lift[i]
        around = (lift[i - 1] if i > 0 else zero) + (lift[i + 1] if i + 1 < rows else zero)
        around = around + jnp.where(lane == 0, 0.0, pltpu.roll(own, 1, 1))
        around = around + jnp.where(lane == width - 1, 0.0, pltpu.roll(own, width - 1, 1))
        both = jnp.concatenate([0.5 * around - 2.0 * own, own * rate_ref[i : i + 1, :]], axis=0)
        prod = mm_nt(both, state_ref[:, i, :])
        total = total + prod[:8] + mm_nt(own, source_ref[:, i, :])
        reacted = reacted + prod[8:]
    total = total - mm(reacted, jac_ref[...])
    edge = mm_nt(lift[0], before_ref[...]) + mm_nt(lift[-1], after_ref[...])
    first = jnp.concatenate([own[:, :1] for own in lift], axis=1)
    last = jnp.concatenate([own[:, width - 1 :] for own in lift], axis=1)
    edge = edge + mm_nt(first, sides_ref[chans:, :]) + mm_nt(last, sides_ref[:chans, :])
    total = total + 0.5 * edge
    out = [jnp.concatenate([total[2 * i : 2 * i + 1], total[2 * i + 1 : 2 * i + 2]], axis=1) for i in range(seps // 2)]
    out.append(jnp.zeros((8 - seps // 2, lanes), jnp.float32))
    f_ref[...] = jnp.concatenate(out, axis=0)


def edges_kernel(state_ref, top_ref, bottom_ref, sides_ref):
    chans, rows, cells = state_ref.shape
    top_ref[...] = state_ref[:, 0, :]
    bottom_ref[...] = state_ref[:, rows - 1, :]
    left = jnp.concatenate([state_ref[:, i, :1] for i in range(rows)], axis=1)
    right = jnp.concatenate([state_ref[:, i, cells - 1 :] for i in range(rows)], axis=1)
    sides_ref[...] = jnp.concatenate([left, right], axis=0)


def order(upper, own, other):
    return jnp.where(upper, other, own), jnp.where(upper, own, other)


def first_kernel(upper_ref, own_ref, other_ref, ss_ref, inv_ref, xt_ref):
    half = own_ref.shape[0] // 2
    upper = upper_ref[0] != 0
    inverse = invert_whole(own_ref[half:, half:] + other_ref[half:, half:])
    inv_ref[...] = inverse
    _, os2 = order(upper, own_ref[:half, half:], other_ref[:half, half:])
    _, oo2 = order(upper, own_ref[:half, :half], other_ref[:half, :half])
    xt2 = mm(os2, inverse)
    xt_ref[...] = xt2
    ss_ref[...] = pack_symmetric(oo2 - mm_nt(xt2, os2))


def factor_kernel(own_ref, other_ref, inv_ref):
    inv_ref[...] = invert(unpack_symmetric(own_ref[...] + other_ref[...]))


def shared_kernel(upper_ref, inv_ref, own_ref, other_ref, ss_ref, xt_ref):
    half = inv_ref.shape[0]
    full = half * 3 // 2
    upper = upper_ref[0] != 0
    _, oo2 = order(upper, own_ref[:half, :], other_ref[:half, :])
    _, os2 = order(upper, own_ref[half : half + full, :], other_ref[half : half + full, :])
    os2 = unpack_full(os2)
    xt2 = mm(os2, inv_ref[...])
    xt_ref[...] = xt2
    ss_ref[...] = oo2 - pack_symmetric(mm_nt(xt2, os2))


def merge(upper, inverse, xt2, os1, os2, own_f, other_f):
    half = inverse.shape[0]
    own, other = to_row(own_f), to_row(other_f)
    first, second = order(upper, own, other)
    shared = own[:, half:] + other[:, half:]
    outer = jnp.concatenate([first[:, :half], second[:, :half]], axis=1)
    xt = mm(jnp.concatenate([os1, jnp.broadcast_to(shared, (8, half))], axis=0), inverse)
    z = xt[half : half + 1]
    both = mm_nt(xt, jnp.concatenate([os1, os2], axis=0))
    cross = -both[:half, half:]
    f = outer - both[half : half + 1]
    return jnp.concatenate([xt[:half], xt2], axis=0), z, both[:half, :half], cross, f


def put_rest(rest_ref, oo, cross, f):
    half = cross.shape[0]
    full = half * 3 // 2
    rest_ref[:half, :] = oo
    rest_ref[half : half + full, :] = pack_full(cross)
    rest_ref[half + full :, :] = from_row(f)


def first_rest_kernel(upper_ref, inv_ref, xt2_ref, own_ref, other_ref, own_f_ref, other_f_ref, rest_ref, xt_ref, z_ref):
    half = inv_ref.shape[0]
    upper = upper_ref[0] != 0
    os1, os2 = order(upper, own_ref[:half, half:], other_ref[:half, half:])
    oo1, _ = order(upper, own_ref[:half, :half], other_ref[:half, :half])
    xt_ref[...], z_ref[...], less, cross, f = merge(
        upper, inv_ref[...], xt2_ref[...], os1, os2, own_f_ref[...], other_f_ref[...]
    )
    put_rest(rest_ref, pack_symmetric(oo1 - less), cross, f)


def unpacked(upper, own_ref, other_ref, half):
    full = half * 3 // 2
    oo1, oo2 = order(upper, own_ref[:half, :], other_ref[:half, :])
    os1, os2 = order(upper, own_ref[half : half + full, :], other_ref[half : half + full, :])
    return unpack_full(os1), unpack_full(os2), oo1, oo2, own_ref[half + full :, :], other_ref[half + full :, :]


def rest_kernel(upper_ref, inv_ref, xt2_ref, own_ref, other_ref, rest_ref, xt_ref, z_ref):
    upper = upper_ref[0] != 0
    os1, os2, oo1, _, own_f, other_f = unpacked(upper, own_ref, other_ref, inv_ref.shape[0])
    xt_ref[...], z_ref[...], less, cross, f = merge(
        upper, inv_ref[...], xt2_ref[...], os1, os2, own_f, other_f
    )
    put_rest(rest_ref, oo1 - pack_symmetric(less), cross, f)


def end_kernel(upper_ref, inv_ref, own_ref, other_ref, t_ref, xt_ref, z_ref, yt_ref, w_ref):
    half = inv_ref.shape[0]
    upper = upper_ref[0] != 0
    os1, os2, oo1, oo2, own_f, other_f = unpacked(upper, own_ref, other_ref, half)
    xt2 = mm(os2, inv_ref[...])
    xt, z, less, cross, f = merge(upper, inv_ref[...], xt2, os1, os2, own_f, other_f)
    less_shared = mm_nt(xt2, os2)
    xt_ref[...] = xt
    z_ref[...] = z
    oo = unpack_symmetric(oo1)
    inverse = invert([rows - less[i * panel : (i + 1) * panel] for i, rows in enumerate(oo)])
    stacked = jnp.concatenate([cross.T, jnp.broadcast_to(f[:, :half], (8, half))], axis=0)
    yt = mm(stacked, inverse)
    w = yt[half : half + 1]
    yt_ref[...] = yt[:half]
    w_ref[...] = w
    t_ref[:half, :] = oo2 - pack_symmetric(less_shared + mm(yt[:half], cross))
    rest = jnp.concatenate([f[:, half:] - mm(w, cross), jnp.zeros((1, half), jnp.float32)], axis=1)
    t_ref[half:, :] = from_row(rest)


def compose_kernel(levels, uppers_ref, yt_ref, w_ref, *refs):
    half = yt_ref.shape[0]
    out_ref = refs[-1]
    row = lax.broadcasted_iota(jnp.int32, (half + 8, half), 0)
    col = lax.broadcasted_iota(jnp.int32, (half + 8, half), 1)
    outer = jnp.concatenate([-yt_ref[...], jnp.broadcast_to(w_ref[...], (8, half))], axis=0)
    answer = jnp.concatenate([outer, jnp.where(row == col, 1.0, 0.0)], axis=1)
    for level in reversed(range(levels)):
        inner = jnp.where(row >= half, refs[2 * level + 1][...], 0.0) - mm(answer, refs[2 * level][...])
        outer = jnp.where(uppers_ref[level] != 0, answer[:, half:], answer[:, :half])
        answer = jnp.concatenate([outer, inner], axis=1)
    out_ref[...] = answer


def solve_kernel(own_ref, other_ref, map_ref, out_ref):
    half = map_ref.shape[0] - 8
    total = own_ref[...] + other_ref[...]
    inverse = invert(unpack_symmetric(total[:half]))
    shared = mm(to_row(total[half:])[:, :half], inverse)
    out_ref[...] = mm(shared, map_ref[:half, :]) + map_ref[half : half + 1, :]


smem = pl.BlockSpec(memory_space=pltpu.SMEM)
vmem = pl.BlockSpec(memory_space=pltpu.VMEM)


def call(kernel, name, shapes, micros, *operands, scalars=1):
    outs = tuple(jax.ShapeDtypeStruct(s, jnp.float32) for s in shapes)
    single = len(outs) == 1
    return pl.pallas_call(
        kernel,
        out_shape=outs[0] if single else outs,
        in_specs=[smem] * scalars + [vmem] * (len(operands) - scalars),
        out_specs=vmem if single else tuple(vmem for _ in outs),
        compiler_params=pltpu.CompilerParams(vmem_limit_bytes=32 << 20),
        cost_estimate=pl.CostEstimate(flops=int(micros * 1e9), bytes_accessed=0, transcendentals=0),
        name=name,
    )(*operands)


def partner(array, level):
    count = lax.axis_size(everywhere)
    return lax.ppermute(array, everywhere, [(i, i ^ 1 << level) for i in range(count)])


def halos(state):
    chans, rows, cells = state.shape
    axial, azim = lax.axis_size("axial"), lax.axis_size("azim")
    top, bottom, sides = call(
        edges_kernel, "edges", [(chans, cells), (chans, cells), (2 * chans, rows)], 0.5, state, scalars=0
    )
    up = [(i, i + 1) for i in range(axial - 1)]
    before = lax.ppermute(bottom, "axial", up)
    after = lax.ppermute(top, "axial", [(j, i) for i, j in up])
    around = [(i, (i + 1) % azim) for i in range(azim)]
    if azim == 2:
        sides = lax.ppermute(sides, "azim", around)
    else:
        left = lax.ppermute(sides[chans:], "azim", around)
        right = lax.ppermute(sides[:chans], "azim", [(j, i) for i, j in around])
        sides = jnp.concatenate([right, left], axis=0)
    return before, after, sides


def body(adjoint_state, adjoint_source, reaction_rate, jacobian, lifting, separator, leaf_schur):
    chans, rows, cells = adjoint_state.shape[1:]
    width = leaf_schur.shape[-1]
    half = width // 2
    full = half * 3 // 2
    levels = lax.axis_size(everywhere).bit_length() - 1
    flat_index = lax.axis_index(everywhere)
    uppers = jnp.bitwise_and(jnp.right_shift(flat_index, jnp.arange(levels, dtype=jnp.int32)), 1)
    upper = [uppers[i : i + 1] for i in range(levels)]
    rest_shapes = [(half + full + 8, lanes), (width, half), (1, half)]

    schur = leaf_schur.reshape(width, width)
    other_schur = partner(schur, 0)
    state = adjoint_state.reshape(chans, rows, cells)
    edges = halos(state)
    ss, inverse, xt2 = call(
        first_kernel, "factor_0", [(half, lanes), (half, half), (half, half)], 8.0, upper[0], schur, other_schur
    )
    other_ss = partner(ss, 1)
    f = call(
        leaf_kernel,
        "leaf_rhs",
        [(8, lanes)],
        2.3,
        separator.reshape(-1),
        ss,
        state,
        adjoint_source.reshape(chans, rows, cells),
        reaction_rate.reshape(rows, cells),
        jacobian.reshape(chans, chans),
        lifting.reshape(-1, rows, cells),
        *edges,
    )
    rest, xt, z = call(
        first_rest_kernel, "rest_0", rest_shapes, 0.05, upper[0], inverse, xt2, schur, other_schur, f, partner(f, 0)
    )
    other_rest = partner(rest, 1)
    saved = [xt, z]
    for level in range(1, levels - 1):
        inverse = call(factor_kernel, f"factor_{level}", [(half, half)], 6.5, ss, other_ss, scalars=0)
        if level < levels - 2:
            ss, xt2 = call(
                shared_kernel,
                f"shared_{level}",
                [(half, lanes), (half, half)],
                1.5,
                upper[level],
                inverse,
                rest,
                other_rest,
            )
            other_ss = partner(ss, level + 1)
            rest, xt, z = call(
                rest_kernel, f"rest_{level}", rest_shapes, 0.05, upper[level], inverse, xt2, rest, other_rest
            )
            other_rest = partner(rest, level + 1)
        else:
            end, xt, z, yt, w = call(
                end_kernel,
                f"end_{level}",
                [(half + 8, lanes), (width, half), (1, half), (half, half), (1, half)],
                9.5,
                upper[level],
                inverse,
                rest,
                other_rest,
            )
        saved += [xt, z]
    other_end = partner(end, levels - 1)
    composed = call(
        functools.partial(compose_kernel, levels - 1), "compose", [(half + 8, width)], 3.7, uppers, yt, w, *saved
    )
    answer = call(solve_kernel, "solve", [(1, width)], 7.0, end, other_end, composed, scalars=0)
    return answer.reshape(1, 1, 1, width)


def solution(mesh):
    in_specs = (
        P("bank", None, "axial", "azim"),
        P("bank", None, "axial", "azim"),
        P("bank", "axial", "azim"),
        P("bank", None, None),
        P("bank", None, "axial", "azim"),
        P("axial", "azim", "bank", None),
        P("axial", "azim", "bank", None, None),
    )
    out_specs = P("axial", "azim", "bank", None)
    return jax.shard_map(body, mesh=mesh, in_specs=in_specs, out_specs=out_specs, check_vma=False)
```

```python
import functools

import jax
import jax.numpy as jnp
from jax import lax
from jax.experimental import pallas as pl
from jax.experimental.pallas import tpu as pltpu
from jax.sharding import PartitionSpec as P

highest = lax.Precision.HIGHEST
high = lax.Precision.HIGH
everywhere = ("axial", "azim", "bank")
panel = 64
lanes = 128


def mm(a, b, precision=highest):
    return jnp.dot(a, b, precision=precision, preferred_element_type=jnp.float32)


def mm_nt(a, b, precision=highest):
    dims = (((1,), (1,)), ((), ()))
    return lax.dot_general(a, b, dims, precision=precision, preferred_element_type=jnp.float32)


def sweep_panel(groups, first, forget=False):
    n = len(groups)
    groups = [list(g) for g in groups]
    widths = [t.shape[1] for t in groups[0]]
    row = lax.broadcasted_iota(jnp.int32, (8, lanes), 0)
    lane_of = [lax.broadcasted_iota(jnp.int32, (8, w), 1) for w in widths]
    row_of = [lax.broadcasted_iota(jnp.int32, (8, w), 0) for w in widths]

    def columns(q, s):
        tile, lane = divmod(first + 8 * s, lanes)
        return [jnp.broadcast_to(groups[q][tile][:, lane + m : lane + m + 1], (8, lanes)) for m in range(8)]

    def across(column, tile):
        return column if widths[tile] == lanes else column[:, : widths[tile]]

    def spread(value, i):
        return jnp.broadcast_to(value[i : i + 1], value.shape)

    def inside(s):
        tile, lane = divmod(first + 8 * s, lanes)
        return tile, lane, (lane_of[tile] >= lane) & (lane_of[tile] < lane + 8)

    def update(q, s, cols, solved):
        home, _, here = inside(s)
        new = []
        for k, tile in enumerate(groups[q]):
            if solved[k] is None:
                new.append(tile)
                continue
            value = jnp.where(here, 0.0, tile) if k == home else tile
            for m in range(8):
                value = value - across(cols[m], k) * spread(solved[k], m)
            new.append(value)
        groups[q] = new

    diag = columns(0, 0)
    cols = {q: columns(q, 0) for q in range(1, n)}
    pending = []
    for s in range(n):
        more = s + 1 < n
        if more:
            low, after = list(cols[s + 1]), columns(s + 1, s + 1)
        home, lane, here = inside(s)
        own = list(groups[s])
        live = [k for k in range(len(own)) if not forget or (k + 1) * lanes > first + 8 * s]
        own[home] = jnp.where(here, jnp.where(lane_of[home] - lane == row_of[home], 1.0, 0.0), own[home])
        scale = None
        for p in range(8):
            inverse = 1.0 / spread(diag[p], p)
            scale = inverse if scale is None else jnp.where(row == p, inverse, scale)
            factor = jnp.where(row == p, 0.0, diag[p] * inverse)
            if more:
                low_factor = low[p] * inverse
            for j in range(p + 1, 8):
                entry = spread(diag[j], p)
                diag[j] = diag[j] - factor * entry
                if more:
                    low[j] = low[j] - low_factor * entry
            if more:
                for j in range(8):
                    after[j] = after[j] - low_factor * spread(low[p], j)
            for k in live:
                own[k] = own[k] - across(factor, k) * spread(own[k], p)
            if pending:
                q, *rest = pending.pop(0)
                update(q, *rest)
                cols[q] = columns(q, s)
        solved = [tile * across(scale, k) if k in live else None for k, tile in enumerate(own)]
        groups[s] = [own[k] if tile is None else tile for k, tile in enumerate(solved)]
        for q in list(range(s + 1, n)) + list(range(s)):
            if s < q < s + 3:
                update(q, s, cols[q], solved)
            else:
                pending.append((q, s, cols[q], solved))
        if more:
            diag = after
            cols[s] = columns(s, s + 1)
            if s + 2 < n:
                cols[s + 2] = columns(s + 2, s + 1)
    for work in pending:
        update(*work)
    return groups


def invert(slabs, forget=False):
    slabs = list(slabs)
    n = slabs[0].shape[1]
    lane = lax.broadcasted_iota(jnp.int32, (1, n), 1)
    for p in range(len(slabs)):
        lo = p * panel
        w = slabs[p]
        groups = [[w[i : i + 8, t : min(t + lanes, n)] for t in range(0, n, lanes)] for i in range(0, panel, 8)]
        groups = sweep_panel(groups, lo, forget)
        w = jnp.concatenate([jnp.concatenate(g, axis=1) for g in groups], axis=0)
        slabs[p] = w
        here = (lane >= lo) & (lane < lo + panel)
        for q in list(range(p + 1, len(slabs))) + list(range(p)):
            if forget and p + 1 == len(slabs):
                slabs[q] = slabs[q][:, -lanes:] - mm(slabs[q][:, lo : lo + panel], w[:, -lanes:])
            else:
                slabs[q] = jnp.where(here, 0.0, slabs[q]) - mm(slabs[q][:, lo : lo + panel], w)
    return jnp.concatenate([slab[:, -lanes:] if forget else slab for slab in slabs], axis=0)


def invert_whole(a):
    return invert([a[i : i + panel] for i in range(0, a.shape[0], panel)])


def pack_symmetric(m):
    third = m.shape[0] // 3
    low = jnp.concatenate([m[:third, 2 * third :], m[2 * third :, 2 * third :]], axis=1)
    return jnp.concatenate([m[:third, : 2 * third], m[third : 2 * third, third:], low], axis=0)


def unpack_symmetric(p):
    third = p.shape[0] // 3
    top, mid, low = p[:third], p[third : 2 * third], p[2 * third :]
    return [
        jnp.concatenate([top, low[:, :third]], axis=1),
        jnp.concatenate([top[:, third:].T, mid], axis=1),
        jnp.concatenate([low[:, :third].T, mid[:, third:].T, low[:, third:]], axis=1),
    ]


def pack_full(m):
    half = m.shape[0] // 2
    tail = jnp.concatenate([m[:half, lanes:], m[half:, lanes:]], axis=1)
    return jnp.concatenate([m[:, :lanes], tail], axis=0)


def unpack_full(p):
    n = p.shape[0] * 2 // 3
    tail = p[n:]
    rest = jnp.concatenate([tail[:, : lanes // 2], tail[:, lanes // 2 :]], axis=0)
    return jnp.concatenate([p[:n], rest], axis=1)


def to_row(f):
    return jnp.concatenate([f[i : i + 1] for i in range(3)], axis=1)


def from_row(row):
    parts = [row[:, i * lanes : (i + 1) * lanes] for i in range(3)]
    return jnp.concatenate(parts + [jnp.zeros((5, lanes), jnp.float32)], axis=0)


def leaf_kernel(sep_ref, after_this_ref, state_ref, source_ref, rate_ref, jac_ref, lift_ref, before_ref, after_ref, sides_ref, f_ref):
    seps = sep_ref.shape[1]
    rows = rate_ref.shape[0]
    width = rate_ref.shape[1]
    chans = jac_ref.shape[0]
    lane = lax.broadcasted_iota(jnp.int32, (8, width), 1)
    c_of = lax.broadcasted_iota(jnp.int32, (8, seps), 0)
    own_c = c_of == lax.broadcasted_iota(jnp.int32, (8, seps), 1)
    where = jnp.max(jnp.where(own_c, sep_ref[...], -1), axis=1, keepdims=True)
    lift = []
    for i in range(rows):
        own = lift_ref[:, i, :]
        own = jnp.concatenate([own, jnp.zeros((8 - seps, width), jnp.float32)], axis=0)
        lift.append(own + jnp.where(where == lane + i * width, 1.0, 0.0))
    zero = jnp.zeros((8, width), jnp.float32)
    mixed = []
    for i in range(rows):
        own = lift[i]
        around = (lift[i - 1] if i > 0 else zero) + (lift[i + 1] if i + 1 < rows else zero)
        around = around + jnp.where(lane == 0, 0.0, pltpu.roll(own, 1, 1))
        around = around + jnp.where(lane == width - 1, 0.0, pltpu.roll(own, width - 1, 1))
        mixed.append(jnp.concatenate([0.5 * around - 2.0 * own, own * rate_ref[i : i + 1, :]], axis=0))
    state = jnp.concatenate([state_ref[:, i, :] for i in range(rows)], axis=1)
    source = jnp.concatenate([source_ref[:, i, :] for i in range(rows)], axis=1)
    prod = mm_nt(jnp.concatenate(mixed, axis=1), state, high)
    first = jnp.concatenate([own[:, :1] for own in lift], axis=1)
    last = jnp.concatenate([own[:, width - 1 :] for own in lift], axis=1)
    edge = mm_nt(lift[0], before_ref[...], high) + mm_nt(lift[-1], after_ref[...], high)
    edge = edge + mm_nt(first, sides_ref[chans:, :], high) + mm_nt(last, sides_ref[:chans, :], high)
    total = prod[:8] + mm_nt(jnp.concatenate(lift, axis=1), source, high)
    total = total - mm(prod[8:], jac_ref[...], high) + 0.5 * edge
    out = [jnp.concatenate([total[2 * i : 2 * i + 1], total[2 * i + 1 : 2 * i + 2]], axis=1) for i in range(seps // 2)]
    out.append(jnp.zeros((8 - seps // 2, lanes), jnp.float32))
    f_ref[...] = jnp.concatenate(out, axis=0)


def edges_kernel(state_ref, top_ref, bottom_ref, sides_ref):
    rows, cells = state_ref.shape[1:]
    top_ref[...] = state_ref[:, 0, :]
    bottom_ref[...] = state_ref[:, rows - 1, :]
    left = jnp.concatenate([state_ref[:, i, :1] for i in range(rows)], axis=1)
    right = jnp.concatenate([state_ref[:, i, cells - 1 :] for i in range(rows)], axis=1)
    sides_ref[...] = jnp.concatenate([left, right], axis=0)


def is_upper(level):
    return jnp.bitwise_and(jnp.right_shift(lax.axis_index(everywhere), level), 1) != 0


def order(upper, own, other):
    return jnp.where(upper, other, own), jnp.where(upper, own, other)


def first_kernel(own_ref, other_ref, ss_ref, inv_ref, xt_ref):
    half = own_ref.shape[0] // 2
    upper = is_upper(0)
    inverse = invert_whole(own_ref[half:, half:] + other_ref[half:, half:])
    inv_ref[...] = inverse
    _, os2 = order(upper, own_ref[:half, half:], other_ref[:half, half:])
    _, oo2 = order(upper, own_ref[:half, :half], other_ref[:half, :half])
    xt2 = mm(os2, inverse)
    xt_ref[...] = xt2
    ss_ref[...] = pack_symmetric(oo2 - mm_nt(xt2, os2))


def factor_kernel(own_ref, other_ref, inv_ref):
    inv_ref[...] = invert(unpack_symmetric(own_ref[...] + other_ref[...]))


def shared_kernel(level, inv_ref, own_ref, other_ref, ss_ref, xt_ref):
    half = inv_ref.shape[0]
    full = half * 3 // 2
    upper = is_upper(level)
    _, oo2 = order(upper, own_ref[:half, :], other_ref[:half, :])
    _, os2 = order(upper, own_ref[half : half + full, :], other_ref[half : half + full, :])
    os2 = unpack_full(os2)
    xt2 = mm(os2, inv_ref[...])
    xt_ref[...] = xt2
    ss_ref[...] = oo2 - pack_symmetric(mm_nt(xt2, os2))


def split_rhs(upper, own_f, other_f):
    own, other = to_row(own_f), to_row(other_f)
    first, second = order(upper, own, other)
    half = own.shape[1] // 2
    return own[:, half:] + other[:, half:], jnp.concatenate([first[:, :half], second[:, :half]], axis=1)


def merge(upper, inverse, xt2, os1, os2, own_f, other_f):
    half = inverse.shape[0]
    shared, outer = split_rhs(upper, own_f, other_f)
    xt = mm(jnp.concatenate([os1, jnp.broadcast_to(shared, (8, half))], axis=0), inverse)
    z = xt[half : half + 1]
    both = mm_nt(xt, jnp.concatenate([os1, os2], axis=0))
    cross = -both[:half, half:]
    f = outer - both[half : half + 1]
    return jnp.concatenate([xt[:half], xt2], axis=0), z, both[:half, :half], cross, f


def put_rest(rest_ref, oo, cross, f):
    half = cross.shape[0]
    full = half * 3 // 2
    rest_ref[:half, :] = oo
    rest_ref[half : half + full, :] = pack_full(cross)
    rest_ref[half + full :, :] = from_row(f)


def first_rest_kernel(inv_ref, xt2_ref, own_ref, other_ref, own_f_ref, other_f_ref, rest_ref, xt_ref, z_ref):
    half = inv_ref.shape[0]
    upper = is_upper(0)
    os1, os2 = order(upper, own_ref[:half, half:], other_ref[:half, half:])
    oo1, _ = order(upper, own_ref[:half, :half], other_ref[:half, :half])
    xt_ref[...], z_ref[...], less, cross, f = merge(
        upper, inv_ref[...], xt2_ref[...], os1, os2, own_f_ref[...], other_f_ref[...]
    )
    put_rest(rest_ref, pack_symmetric(oo1 - less), cross, f)


def unpacked(upper, own_ref, other_ref, half):
    full = half * 3 // 2
    oo1, oo2 = order(upper, own_ref[:half, :], other_ref[:half, :])
    os1, os2 = order(upper, own_ref[half : half + full, :], other_ref[half : half + full, :])
    return unpack_full(os1), unpack_full(os2), oo1, oo2, own_ref[half + full :, :], other_ref[half + full :, :]


def rest_kernel(level, inv_ref, xt2_ref, own_ref, other_ref, rest_ref, xt_ref, z_ref):
    upper = is_upper(level)
    os1, os2, oo1, _, own_f, other_f = unpacked(upper, own_ref, other_ref, inv_ref.shape[0])
    xt_ref[...], z_ref[...], less, cross, f = merge(
        upper, inv_ref[...], xt2_ref[...], os1, os2, own_f, other_f
    )
    put_rest(rest_ref, oo1 - pack_symmetric(less), cross, f)


def end_kernel(level, inv_ref, own_ref, other_ref, t_ref, xt_ref, z_ref, yt_ref, w_ref):
    half = inv_ref.shape[0]
    upper = is_upper(level)
    os1, os2, oo1, oo2, own_f, other_f = unpacked(upper, own_ref, other_ref, half)
    xt1 = mm(os1, inv_ref[...])
    less = mm_nt(xt1, os1)
    oo = unpack_symmetric(oo1)
    inverse = invert([rows - less[i * panel : (i + 1) * panel] for i, rows in enumerate(oo)])
    xt2 = mm(os2, inv_ref[...])
    less_shared = mm_nt(xt2, os2)
    shared, outer = split_rhs(upper, own_f, other_f)
    z = mm(shared, inv_ref[...])
    cross = -mm_nt(xt1, os2)
    f = outer - jnp.concatenate([mm_nt(z, os1), mm_nt(z, os2)], axis=1)
    xt_ref[:half, :] = xt1
    xt_ref[half:, :] = xt2
    z_ref[...] = z
    stacked = jnp.concatenate([cross.T, jnp.broadcast_to(f[:, :half], (8, half))], axis=0)
    yt = mm(stacked, inverse)
    w = yt[half : half + 1]
    yt_ref[...] = yt[:half]
    w_ref[...] = w
    t_ref[:half, :] = oo2 - pack_symmetric(less_shared + mm(yt[:half], cross))
    rest = jnp.concatenate([f[:, half:] - mm(w, cross), jnp.zeros((1, half), jnp.float32)], axis=1)
    t_ref[half:, :] = from_row(rest)


def compose_kernel(levels, yt_ref, w_ref, *refs):
    half = yt_ref.shape[0]
    out_ref = refs[-1]
    row = lax.broadcasted_iota(jnp.int32, (half + 8, half), 0)
    col = lax.broadcasted_iota(jnp.int32, (half + 8, half), 1)
    outer = jnp.concatenate([-yt_ref[...], jnp.broadcast_to(w_ref[...], (8, half))], axis=0)
    answer = jnp.concatenate([outer, jnp.where(row == col, 1.0, 0.0)], axis=1)
    for level in reversed(range(levels)):
        inner = jnp.where(row >= half, refs[2 * level + 1][...], 0.0) - mm(answer, refs[2 * level][...])
        outer = jnp.where(is_upper(level), answer[:, half:], answer[:, :half])
        answer = jnp.concatenate([outer, inner], axis=1)
    out_ref[...] = answer


def solve_kernel(own_ref, other_ref, map_ref, out_ref):
    half = map_ref.shape[0] - 8
    width = map_ref.shape[1]
    total = own_ref[...] + other_ref[...]
    right = jnp.broadcast_to(to_row(total[half:])[:, :half], (8, half)).T
    pad = jnp.zeros((panel, lanes - half % lanes - 8), jnp.float32)
    slabs = [
        jnp.concatenate([rows, right[i * panel : (i + 1) * panel], pad], axis=1)
        for i, rows in enumerate(unpack_symmetric(total[:half]))
    ]
    shared = invert(slabs, forget=True)[:, half % lanes : half % lanes + 1]
    parts = jnp.broadcast_to(shared, (half, width)) * map_ref[:half, :]
    out_ref[...] = jnp.sum(parts, axis=0, keepdims=True) + map_ref[half : half + 1, :]


vmem = pl.BlockSpec(memory_space=pltpu.VMEM)


def call(kernel, name, shapes, micros, *operands):
    outs = tuple(jax.ShapeDtypeStruct(s, jnp.float32) for s in shapes)
    single = len(outs) == 1
    return pl.pallas_call(
        kernel,
        out_shape=outs[0] if single else outs,
        in_specs=[vmem] * len(operands),
        out_specs=vmem if single else tuple(vmem for _ in outs),
        compiler_params=pltpu.CompilerParams(vmem_limit_bytes=32 << 20),
        cost_estimate=pl.CostEstimate(flops=int(micros * 1e9), bytes_accessed=0, transcendentals=0),
        name=name,
    )(*operands)


def partner(array, level):
    count = lax.axis_size(everywhere)
    return lax.ppermute(array, everywhere, [(i, i ^ 1 << level) for i in range(count)])


def halos(state):
    chans, rows, cells = state.shape
    axial, azim = lax.axis_size("axial"), lax.axis_size("azim")
    top, bottom, sides = call(
        edges_kernel, "edges", [(chans, cells), (chans, cells), (2 * chans, rows)], 0.5, state
    )
    up = [(i, i + 1) for i in range(axial - 1)]
    before = lax.ppermute(bottom, "axial", up)
    after = lax.ppermute(top, "axial", [(j, i) for i, j in up])
    around = [(i, (i + 1) % azim) for i in range(azim)]
    if azim == 2:
        sides = lax.ppermute(sides, "azim", around)
    else:
        left = lax.ppermute(sides[chans:], "azim", around)
        right = lax.ppermute(sides[:chans], "azim", [(j, i) for i, j in around])
        sides = jnp.concatenate([right, left], axis=0)
    return before, after, sides


def body(adjoint_state, adjoint_source, reaction_rate, jacobian, lifting, separator, leaf_schur):
    chans, rows, cells = adjoint_state.shape[1:]
    width = leaf_schur.shape[-1]
    half = width // 2
    full = half * 3 // 2
    levels = lax.axis_size(everywhere).bit_length() - 1
    rest_shapes = [(half + full + 8, lanes), (width, half), (1, half)]

    schur = leaf_schur.reshape(width, width)
    other_schur = partner(schur, 0)
    state = adjoint_state.reshape(chans, rows, cells)
    edges = halos(state)
    ss, inverse, xt2 = call(
        first_kernel, "factor_0", [(half, lanes), (half, half), (half, half)], 8.0, schur, other_schur
    )
    other_ss = partner(ss, 1)
    f = call(
        leaf_kernel,
        "leaf_rhs",
        [(8, lanes)],
        2.3,
        separator.reshape(1, -1),
        ss,
        state,
        adjoint_source.reshape(chans, rows, cells),
        reaction_rate.reshape(rows, cells),
        jacobian.reshape(chans, chans),
        lifting.reshape(-1, rows, cells),
        *edges,
    )
    rest, xt, z = call(
        first_rest_kernel, "rest_0", rest_shapes, 0.05, inverse, xt2, schur, other_schur, f, partner(f, 0)
    )
    other_rest = partner(rest, 1)
    saved = [xt, z]
    for level in range(1, levels - 1):
        inverse = call(factor_kernel, f"factor_{level}", [(half, half)], 6.5, ss, other_ss)
        if level < levels - 2:
            ss, xt2 = call(
                functools.partial(shared_kernel, level),
                f"shared_{level}",
                [(half, lanes), (half, half)],
                1.5,
                inverse,
                rest,
                other_rest,
            )
            other_ss = partner(ss, level + 1)
            rest, xt, z = call(
                functools.partial(rest_kernel, level), f"rest_{level}", rest_shapes, 0.05, inverse, xt2, rest, other_rest
            )
            other_rest = partner(rest, level + 1)
        else:
            end, xt, z, yt, w = call(
                functools.partial(end_kernel, level),
                f"end_{level}",
                [(half + 8, lanes), (width, half), (1, half), (half, half), (1, half)],
                9.5,
                inverse,
                rest,
                other_rest,
            )
        saved += [xt, z]
    other_end = partner(end, levels - 1)
    composed = call(
        functools.partial(compose_kernel, levels - 1), "compose", [(half + 8, width)], 3.7, yt, w, *saved
    )
    answer = call(solve_kernel, "solve", [(1, width)], 7.0, end, other_end, composed)
    return answer.reshape(1, 1, 1, width)


def solution(mesh):
    in_specs = (
        P("bank", None, "axial", "azim"),
        P("bank", None, "axial", "azim"),
        P("bank", "axial", "azim"),
        P("bank", None, None),
        P("bank", None, "axial", "azim"),
        P("axial", "azim", "bank", None),
        P("axial", "azim", "bank", None, None),
    )
    out_specs = P("axial", "azim", "bank", None)
    return jax.shard_map(body, mesh=mesh, in_specs=in_specs, out_specs=out_specs, check_vma=False)
```

```python
import functools

import jax
import jax.numpy as jnp
from jax import lax
from jax.experimental import pallas as pl
from jax.experimental.pallas import tpu as pltpu
from jax.sharding import PartitionSpec as P

highest = lax.Precision.HIGHEST
high = lax.Precision.HIGH
everywhere = ("axial", "azim", "bank")
lanes = 128


def mm(a, b, precision=highest):
    return jnp.dot(a, b, precision=precision, preferred_element_type=jnp.float32)


def mm_nt(a, b, precision=highest):
    dims = (((1,), (1,)), ((), ()))
    return lax.dot_general(a, b, dims, precision=precision, preferred_element_type=jnp.float32)


def mm_tn(a, b, precision=highest):
    dims = (((0,), (0,)), ((), ()))
    return lax.dot_general(a, b, dims, precision=precision, preferred_element_type=jnp.float32)


def sweep_panel(groups, first, jobs):
    n = len(groups)
    groups = [list(g) for g in groups]
    widths = [t.shape[1] for t in groups[0]]
    row = lax.broadcasted_iota(jnp.int32, (8, lanes), 0)
    lane_of = [lax.broadcasted_iota(jnp.int32, (8, w), 1) for w in widths]
    row_of = [lax.broadcasted_iota(jnp.int32, (8, w), 0) for w in widths]

    def columns(q, s):
        tile, lane = divmod(first + 8 * s, lanes)
        return [jnp.broadcast_to(groups[q][tile][:, lane + m : lane + m + 1], (8, lanes)) for m in range(8)]

    def across(column, tile):
        return column if widths[tile] == lanes else column[:, : widths[tile]]

    def spread(value, i):
        return jnp.broadcast_to(value[i : i + 1], value.shape)

    def inside(s):
        tile, lane = divmod(first + 8 * s, lanes)
        return tile, lane, (lane_of[tile] >= lane) & (lane_of[tile] < lane + 8)

    def update(q, s, cols, solved):
        home, _, here = inside(s)
        new = []
        for k, tile in enumerate(groups[q]):
            value = jnp.where(here, 0.0, tile) if k == home else tile
            for m in range(8):
                value = value - across(cols[m], k) * spread(solved[k], m)
            new.append(value)
        groups[q] = new

    diag = columns(0, 0)
    cols = {q: columns(q, 0) for q in range(1, n)}
    pending, before, after = [], [], []
    for s in range(n):
        more = s + 1 < n
        if more:
            low, ahead = list(cols[s + 1]), columns(s + 1, s + 1)
        home, lane, here = inside(s)
        own = list(groups[s])
        own[home] = jnp.where(here, jnp.where(lane_of[home] - lane == row_of[home], 1.0, 0.0), own[home])
        before.append(list(own))
        scale = None
        for p in range(8):
            inverse = 1.0 / spread(diag[p], p)
            scale = inverse if scale is None else jnp.where(row == p, inverse, scale)
            factor = jnp.where(row == p, 0.0, diag[p] * inverse)
            if more:
                low_factor = low[p] * inverse
            for j in range(p + 1, 8):
                entry = spread(diag[j], p)
                diag[j] = diag[j] - factor * entry
                if more:
                    low[j] = low[j] - low_factor * entry
            if more:
                for j in range(8):
                    ahead[j] = ahead[j] - low_factor * spread(low[p], j)
            for k in range(len(own)):
                own[k] = own[k] - across(factor, k) * spread(own[k], p)
            for _ in range(-(-len(pending) // (8 - p))):
                q, *rest = pending.pop(0)
                update(q, *rest)
                cols[q] = columns(q, s)
        solved = [tile * across(scale, k) for k, tile in enumerate(own)]
        after.append(solved)
        for q in range(s + 1, n):
            if q < s + 3:
                update(q, s, cols[q], solved)
            else:
                pending.append((q, s, cols[q], solved))
        if more:
            diag = ahead
            if s + 2 < n:
                cols[s + 2] = columns(s + 2, s + 1)
        if jobs:
            jobs.pop(0)()

    def whole(parts):
        return jnp.concatenate([jnp.concatenate(g, axis=1) for g in parts], axis=0)

    return whole(before), whole(after)


def factorize(a, panel, jobs=()):
    n, m = a.shape
    jobs = list(jobs)
    slabs = [a[i : i + panel] for i in range(0, n, panel)]
    lower, scaled = [], []
    for p in range(len(slabs)):
        lo = p * panel
        w = slabs[p]
        groups = [[w[i : i + 8, t : min(t + lanes, m)] for t in range(0, m, lanes)] for i in range(0, panel, 8)]
        g, r = sweep_panel(groups, lo, jobs)
        lane = lax.broadcasted_iota(jnp.int32, (panel, m), 1)
        row = lax.broadcasted_iota(jnp.int32, (panel, m), 0)
        here = (lane >= lo) & (lane < lo + panel)
        ahead = lane >= lo + row // 8 * 8 + 8
        inner = jnp.where(here & ahead, 0.0, r)
        for q in range(p + 1, len(slabs)):
            slabs[q] = jnp.where(here, 0.0, slabs[q]) - mm_tn(g[:, q * panel : (q + 1) * panel], inner)
        drop = ahead & (lane < n)
        lower.append(jnp.where(drop, 0.0, g))
        scaled.append(jnp.where(drop, 0.0, r))
    for job in jobs:
        job()
    return jnp.concatenate(lower, axis=0), jnp.concatenate(scaled, axis=0)


def pack_symmetric(m):
    third = m.shape[0] // 3
    low = jnp.concatenate([m[:third, 2 * third :], m[2 * third :, 2 * third :]], axis=1)
    return jnp.concatenate([m[:third, : 2 * third], m[third : 2 * third, third:], low], axis=0)


def unpack_symmetric(p):
    third = p.shape[0] // 3
    top, mid, low = p[:third], p[third : 2 * third], p[2 * third :]
    rows = [
        jnp.concatenate([top, low[:, :third]], axis=1),
        jnp.concatenate([top[:, third:].T, mid], axis=1),
        jnp.concatenate([low[:, :third].T, mid[:, third:].T, low[:, third:]], axis=1),
    ]
    return jnp.concatenate(rows, axis=0)


def pack_full(m):
    half = m.shape[0] // 2
    tail = jnp.concatenate([m[:half, lanes:], m[half:, lanes:]], axis=1)
    return jnp.concatenate([m[:, :lanes], tail], axis=0)


def unpack_full(p):
    n = p.shape[0] * 2 // 3
    tail = p[n:]
    rest = jnp.concatenate([tail[:, : lanes // 2], tail[:, lanes // 2 :]], axis=0)
    return jnp.concatenate([p[:n], rest], axis=1)


def to_row(f):
    return jnp.concatenate([f[i : i + 1] for i in range(3)], axis=1)


def from_row(row):
    parts = [row[:, i * lanes : (i + 1) * lanes] for i in range(3)]
    return jnp.concatenate(parts + [jnp.zeros((5, lanes), jnp.float32)], axis=0)


def leaf_kernel(where_ref, after_this_ref, state_ref, source_ref, rate_ref, jac_ref, lift_ref, before_ref, after_ref, sides_ref, f_ref):
    seps = lift_ref.shape[0]
    rows = rate_ref.shape[0]
    width = rate_ref.shape[1]
    chans = jac_ref.shape[0]
    lane = lax.broadcasted_iota(jnp.int32, (8, width), 1)
    where = where_ref[:, :1].astype(jnp.int32)
    lift = []
    for i in range(rows):
        own = lift_ref[:, i, :]
        own = jnp.concatenate([own, jnp.zeros((8 - seps, width), jnp.float32)], axis=0)
        lift.append(own + jnp.where(where == lane + i * width, 1.0, 0.0))
    zero = jnp.zeros((8, width), jnp.float32)
    mixed = []
    for i in range(rows):
        own = lift[i]
        around = (lift[i - 1] if i > 0 else zero) + (lift[i + 1] if i + 1 < rows else zero)
        around = around + jnp.where(lane == 0, 0.0, pltpu.roll(own, 1, 1))
        around = around + jnp.where(lane == width - 1, 0.0, pltpu.roll(own, width - 1, 1))
        mixed.append(jnp.concatenate([0.5 * around - 2.0 * own, own * rate_ref[i : i + 1, :]], axis=0))
    state = jnp.concatenate([state_ref[:, i, :] for i in range(rows)], axis=1)
    source = jnp.concatenate([source_ref[:, i, :] for i in range(rows)], axis=1)
    prod = mm_nt(jnp.concatenate(mixed, axis=1), state, high)
    first = jnp.concatenate([own[:, :1] for own in lift], axis=1)
    last = jnp.concatenate([own[:, width - 1 :] for own in lift], axis=1)
    place = lax.axis_index("axial")
    inside = (place > 0, place < lax.axis_size("axial") - 1)
    before, after = [jnp.where(there, ref[...], 0.0) for there, ref in zip(inside, (before_ref, after_ref))]
    edge = mm_nt(lift[0], before, high) + mm_nt(lift[-1], after, high)
    edge = edge + mm_nt(first, sides_ref[chans:, :], high) + mm_nt(last, sides_ref[:chans, :], high)
    total = prod[:8] + mm_nt(jnp.concatenate(lift, axis=1), source, high)
    total = total - mm(prod[8:], jac_ref[...], high) + 0.5 * edge
    out = [jnp.concatenate([total[2 * i : 2 * i + 1], total[2 * i + 1 : 2 * i + 2]], axis=1) for i in range(seps // 2)]
    out.append(jnp.zeros((8 - seps // 2, lanes), jnp.float32))
    f_ref[...] = jnp.concatenate(out, axis=0)


def edges_kernel(state_ref, top_ref, bottom_ref, sides_ref):
    rows, cells = state_ref.shape[1:]
    top_ref[...] = state_ref[:, 0, :]
    bottom_ref[...] = state_ref[:, rows - 1, :]
    left = jnp.concatenate([state_ref[:, i, :1] for i in range(rows)], axis=1)
    right = jnp.concatenate([state_ref[:, i, cells - 1 :] for i in range(rows)], axis=1)
    sides_ref[...] = jnp.concatenate([left, right], axis=0)


def is_upper(level):
    return jnp.bitwise_and(jnp.right_shift(lax.axis_index(everywhere), level), 1) != 0


def order(upper, own, other):
    return jnp.where(upper, other, own), jnp.where(upper, own, other)


def first_kernel(own_ref, other_ref, sep_ref, ss_ref, inv_ref, xt2_ref, where_ref):
    seps = sep_ref.shape[1]
    c_of = lax.broadcasted_iota(jnp.int32, (8, seps), 0)
    own_c = c_of == lax.broadcasted_iota(jnp.int32, (8, seps), 1)
    where = jnp.max(jnp.where(own_c, sep_ref[...], -1), axis=1, keepdims=True)
    where_ref[...] = jnp.broadcast_to(where, (8, lanes)).astype(jnp.float32)
    half = own_ref.shape[0] // 2
    upper = is_upper(0)
    inverse = mm_tn(*factorize(own_ref[half:, half:] + other_ref[half:, half:], half // 3))
    inv_ref[...] = inverse
    _, os2 = order(upper, own_ref[:half, half:], other_ref[:half, half:])
    _, oo2 = order(upper, own_ref[:half, :half], other_ref[:half, :half])
    xt2 = mm(os2, inverse)
    xt2_ref[...] = xt2
    ss_ref[...] = pack_symmetric(oo2 - mm_nt(xt2, os2))


def factor_kernel(own_ref, other_ref, inv_ref):
    inv_ref[...] = mm_tn(*factorize(unpack_symmetric(own_ref[...] + other_ref[...]), own_ref.shape[0] // 3))


def shared_kernel(level, inv_ref, own_ref, other_ref, ss_ref, xt2_ref):
    half = inv_ref.shape[0]
    full = half * 3 // 2
    upper = is_upper(level)
    _, oo2 = order(upper, own_ref[:half, :], other_ref[:half, :])
    _, os2 = order(upper, own_ref[half : half + full, :], other_ref[half : half + full, :])
    os2 = unpack_full(os2)
    xt2 = mm(os2, inv_ref[...])
    xt2_ref[...] = xt2
    ss_ref[...] = oo2 - pack_symmetric(mm_nt(xt2, os2))


def split_rhs(upper, own_f, other_f):
    own, other = to_row(own_f), to_row(other_f)
    first, second = order(upper, own, other)
    half = own.shape[1] // 2
    return own[:, half:] + other[:, half:], jnp.concatenate([first[:, :half], second[:, :half]], axis=1)


def merge(upper, inv_ref, xt2_ref, os1, os2, own_f, other_f, xt_ref, z_ref):
    half = inv_ref.shape[0]
    shared, outer = split_rhs(upper, own_f, other_f)
    xt = mm(jnp.concatenate([os1, jnp.broadcast_to(shared, (8, half))], axis=0), inv_ref[...])
    xt_ref[:half, :] = xt[:half]
    xt_ref[half:, :] = xt2_ref[...]
    z_ref[...] = xt[half : half + 1]
    both = mm_nt(xt, jnp.concatenate([os1, os2], axis=0))
    return both[:half, :half], -both[:half, half:], outer - both[half : half + 1]


def put_rest(rest_ref, oo, cross, f):
    half = cross.shape[0]
    full = half * 3 // 2
    rest_ref[:half, :] = oo
    rest_ref[half : half + full, :] = pack_full(cross)
    rest_ref[half + full :, :] = from_row(f)


def first_rest_kernel(inv_ref, xt2_ref, own_ref, other_ref, own_f_ref, other_f_ref, rest_ref, xt_ref, z_ref):
    half = inv_ref.shape[0]
    upper = is_upper(0)
    os1, os2 = order(upper, own_ref[:half, half:], other_ref[:half, half:])
    oo1, _ = order(upper, own_ref[:half, :half], other_ref[:half, :half])
    less, cross, f = merge(upper, inv_ref, xt2_ref, os1, os2, own_f_ref[...], other_f_ref[...], xt_ref, z_ref)
    put_rest(rest_ref, pack_symmetric(oo1 - less), cross, f)


def unpacked(upper, own_ref, other_ref, half):
    full = half * 3 // 2
    oo1, oo2 = order(upper, own_ref[:half, :], other_ref[:half, :])
    os1, os2 = order(upper, own_ref[half : half + full, :], other_ref[half : half + full, :])
    return os1, os2, oo1, oo2, own_ref[half + full :, :], other_ref[half + full :, :]


def rest_kernel(level, inv_ref, xt2_ref, own_ref, other_ref, rest_ref, xt_ref, z_ref):
    upper = is_upper(level)
    os1, os2, oo1, _, own_f, other_f = unpacked(upper, own_ref, other_ref, inv_ref.shape[0])
    less, cross, f = merge(
        upper, inv_ref, xt2_ref, unpack_full(os1), unpack_full(os2), own_f, other_f, xt_ref, z_ref
    )
    put_rest(rest_ref, oo1 - pack_symmetric(less), cross, f)


def end_kernel(level, inv_ref, own_ref, other_ref, t_ref, xt_ref, z_ref, end_v_ref, end_r_ref, work_ref):
    half = inv_ref.shape[0]
    upper = is_upper(level)
    os1, os2, oo1, oo2, own_f, other_f = unpacked(upper, own_ref, other_ref, half)
    os1 = unpack_full(os1)
    xt1 = mm(os1, inv_ref[...])
    xt_ref[:half, :] = xt1
    piece = half // 3
    os2 = unpack_full(os2)
    done = {}

    def products(i):
        rows = slice(i * piece, (i + 1) * piece)
        xt_ref[half + i * piece : half + (i + 1) * piece, :] = mm(os2[rows], inv_ref[...])

    def crosses(i):
        rows = slice(i * piece, (i + 1) * piece)
        work_ref[rows, :] = mm_nt(os2[rows], xt_ref[...])

    def right():
        shared, outer = split_rhs(upper, own_f, other_f)
        z = mm(jnp.broadcast_to(shared, (8, half)), inv_ref[...])
        z_ref[...] = z[:1]
        done["f"] = outer - mm_nt(z, jnp.concatenate([os1, os2], axis=0))[:1]

    jobs = [functools.partial(products, i) for i in range(3)] + [functools.partial(crosses, i) for i in range(3)]
    g, r = factorize(unpack_symmetric(oo1) - mm_nt(xt1, os1), half // 2, jobs + [right])
    end_r_ref[...] = r
    f = done["f"]
    stacked = jnp.concatenate([-work_ref[:, :half], jnp.broadcast_to(f[:, :half], (8, half))], axis=0)
    vu = mm_nt(stacked, jnp.concatenate([g, r], axis=0))
    end_v_ref[...] = vu[:, :half]
    lost = mm_nt(vu[:, half:], vu[:half, :half])
    t_ref[:half, :] = oo2 - pack_symmetric(work_ref[:, half:] + lost[:half])
    t_ref[half:, :] = from_row(
        jnp.concatenate([f[:, half:] - lost[half : half + 1], jnp.zeros((1, half), jnp.float32)], axis=1)
    )


def compose_kernel(levels, end_v_ref, end_r_ref, *refs):
    half = end_r_ref.shape[0]
    out_ref = refs[-1]
    row = lax.broadcasted_iota(jnp.int32, (half + 8, half), 0)
    col = lax.broadcasted_iota(jnp.int32, (half + 8, half), 1)
    outer = mm(jnp.where(row < half, -end_v_ref[...], end_v_ref[...]), end_r_ref[...])
    answer = jnp.concatenate([outer, jnp.where(row == col, 1.0, 0.0)], axis=1)
    for level in reversed(range(levels)):
        xt_ref, z_ref = refs[2 * level : 2 * level + 2]
        inner = jnp.where(row >= half, z_ref[...], 0.0) - mm(answer, xt_ref[...])
        outer = jnp.where(is_upper(level), answer[:, half:], answer[:, :half])
        answer = jnp.concatenate([outer, inner], axis=1)
    out_ref[...] = answer


def solve_kernel(own_ref, other_ref, map_ref, out_ref):
    half = map_ref.shape[0] - 8
    width = map_ref.shape[1]
    total = own_ref[...] + other_ref[...]
    right = jnp.broadcast_to(to_row(total[half:])[:, :half], (8, half)).T
    pad = jnp.zeros((half, lanes - half % lanes - 8), jnp.float32)
    g, r = factorize(jnp.concatenate([unpack_symmetric(total[:half]), right, pad], axis=1), half // 2)
    shared = jnp.sum(g[:, half : half + 1] * r[:, :half], axis=0, keepdims=True)
    shared = jnp.broadcast_to(shared, (8, half)).T[:, :1]
    parts = jnp.broadcast_to(shared, (half, width)) * map_ref[:half, :]
    out_ref[...] = jnp.sum(parts, axis=0, keepdims=True) + map_ref[half : half + 1, :]


vmem = pl.BlockSpec(memory_space=pltpu.VMEM)


def call(kernel, name, shapes, micros, *operands, scratch=()):
    outs = tuple(jax.ShapeDtypeStruct(s, jnp.float32) for s in shapes)
    single = len(outs) == 1
    return pl.pallas_call(
        kernel,
        out_shape=outs[0] if single else outs,
        in_specs=[vmem] * len(operands),
        out_specs=vmem if single else tuple(vmem for _ in outs),
        scratch_shapes=[pltpu.VMEM(shape, jnp.float32) for shape in scratch],
        compiler_params=pltpu.CompilerParams(vmem_limit_bytes=32 << 20),
        cost_estimate=pl.CostEstimate(flops=int(micros * 1e9), bytes_accessed=0, transcendentals=0),
        name=name,
    )(*operands)


def partner(array, level):
    count = lax.axis_size(everywhere)
    return lax.ppermute(array, everywhere, [(i, i ^ 1 << level) for i in range(count)])


def halos(state):
    chans, rows, cells = state.shape
    axial, azim = lax.axis_size("axial"), lax.axis_size("azim")
    shapes = [(chans, cells), (chans, cells), (2 * chans, rows)]
    top, bottom, sides = call(edges_kernel, "edges", shapes, 0.5, state)
    up = [(i, (i + 1) % axial) for i in range(axial)]
    before = lax.ppermute(bottom, "axial", up)
    after = lax.ppermute(top, "axial", [(j, i) for i, j in up])
    around = [(i, (i + 1) % azim) for i in range(azim)]
    if azim == 2:
        sides = lax.ppermute(sides, "azim", around)
    else:
        left = lax.ppermute(sides[chans:], "azim", around)
        right = lax.ppermute(sides[:chans], "azim", [(j, i) for i, j in around])
        sides = jnp.concatenate([right, left], axis=0)
    return before, after, sides


def body(adjoint_state, adjoint_source, reaction_rate, jacobian, lifting, separator, leaf_schur):
    chans, rows, cells = adjoint_state.shape[1:]
    width = leaf_schur.shape[-1]
    half = width // 2
    full = half * 3 // 2
    levels = lax.axis_size(everywhere).bit_length() - 1
    rest_shapes = [(half + full + 8, lanes), (width, half), (1, half)]
    shared_shapes = [(half, lanes), (half, half)]

    schur = leaf_schur.reshape(width, width)
    other_schur = partner(schur, 0)
    state = adjoint_state.reshape(chans, rows, cells)
    edges = halos(state)
    ss, inverse, xt2, where = call(
        first_kernel,
        "factor_0",
        [(half, lanes), (half, half), (half, half), (8, lanes)],
        8.0,
        schur,
        other_schur,
        separator.reshape(1, -1),
    )
    other_ss = partner(ss, 1)
    f = call(
        leaf_kernel,
        "leaf_rhs",
        [(8, lanes)],
        2.3,
        where,
        ss,
        state,
        adjoint_source.reshape(chans, rows, cells),
        reaction_rate.reshape(rows, cells),
        jacobian.reshape(chans, chans),
        lifting.reshape(-1, rows, cells),
        *edges,
    )
    rest, xt, z = call(
        first_rest_kernel, "rest_0", rest_shapes, 0.05, inverse, xt2, schur, other_schur, f, partner(f, 0)
    )
    other_rest = partner(rest, 1)
    saved = [xt, z]
    for level in range(1, levels - 1):
        inverse = call(factor_kernel, f"factor_{level}", [(half, half)], 6.5, ss, other_ss)
        operands = (rest, other_rest)
        if level < levels - 2:
            ss, xt2 = call(
                functools.partial(shared_kernel, level), f"shared_{level}", shared_shapes, 1.5, inverse, *operands
            )
            other_ss = partner(ss, level + 1)
            rest, xt, z = call(
                functools.partial(rest_kernel, level), f"rest_{level}", rest_shapes, 0.05, inverse, xt2, *operands
            )
            other_rest = partner(rest, level + 1)
        else:
            end, xt, z, end_v, end_r = call(
                functools.partial(end_kernel, level),
                f"end_{level}",
                [(half + 8, lanes), (width, half), (1, half), (half + 8, half), (half, half)],
                9.5,
                inverse,
                *operands,
                scratch=[(half, width)],
            )
        saved += [xt, z]
    other_end = partner(end, levels - 1)
    composed = call(
        functools.partial(compose_kernel, levels - 1), "compose", [(half + 8, width)], 3.7, end_v, end_r, *saved
    )
    answer = call(solve_kernel, "solve", [(1, width)], 7.0, end, other_end, composed)
    return answer.reshape(1, 1, 1, width)


def solution(mesh):
    in_specs = (
        P("bank", None, "axial", "azim"),
        P("bank", None, "axial", "azim"),
        P("bank", "axial", "azim"),
        P("bank", None, None),
        P("bank", None, "axial", "azim"),
        P("axial", "azim", "bank", None),
        P("axial", "azim", "bank", None, None),
    )
    out_specs = P("axial", "azim", "bank", None)
    return jax.shard_map(body, mesh=mesh, in_specs=in_specs, out_specs=out_specs, check_vma=False)
```

```python
import functools

import jax
import jax.numpy as jnp
from jax import lax
from jax.experimental import pallas as pl
from jax.experimental.pallas import tpu as pltpu
from jax.sharding import PartitionSpec as P

highest = lax.Precision.HIGHEST
high = lax.Precision.HIGH
everywhere = ("axial", "azim", "bank")
lanes = 128


def mm(a, b, precision=highest):
    return jnp.dot(a, b, precision=precision, preferred_element_type=jnp.float32)


def mm_nt(a, b, precision=highest):
    dims = (((1,), (1,)), ((), ()))
    return lax.dot_general(a, b, dims, precision=precision, preferred_element_type=jnp.float32)


def mm_tn(a, b, precision=highest):
    dims = (((0,), (0,)), ((), ()))
    return lax.dot_general(a, b, dims, precision=precision, preferred_element_type=jnp.float32)


def sweep_panel(groups, first, jobs):
    n = len(groups)
    groups = [list(g) for g in groups]
    widths = [t.shape[1] for t in groups[0]]
    row = lax.broadcasted_iota(jnp.int32, (8, lanes), 0)
    lane_of = [lax.broadcasted_iota(jnp.int32, (8, w), 1) for w in widths]
    row_of = [lax.broadcasted_iota(jnp.int32, (8, w), 0) for w in widths]

    def columns(q, s):
        tile, lane = divmod(first + 8 * s, lanes)
        return [jnp.broadcast_to(groups[q][tile][:, lane + m : lane + m + 1], (8, lanes)) for m in range(8)]

    def across(column, tile):
        return column if widths[tile] == lanes else column[:, : widths[tile]]

    def spread(value, i):
        return jnp.broadcast_to(value[i : i + 1], value.shape)

    def inside(s):
        tile, lane = divmod(first + 8 * s, lanes)
        return tile, lane, (lane_of[tile] >= lane) & (lane_of[tile] < lane + 8)

    def update(q, s, cols, solved):
        home, _, here = inside(s)
        new = []
        for k, tile in enumerate(groups[q]):
            value = jnp.where(here, 0.0, tile) if k == home else tile
            for m in range(8):
                value = value - across(cols[m], k) * spread(solved[k], m)
            new.append(value)
        groups[q] = new

    diag = columns(0, 0)
    cols = {q: columns(q, 0) for q in range(1, n)}
    pending, before, after = [], [], []
    for s in range(n):
        more = s + 1 < n
        if more:
            low, ahead = list(cols[s + 1]), columns(s + 1, s + 1)
        home, lane, here = inside(s)
        own = list(groups[s])
        own[home] = jnp.where(here, jnp.where(lane_of[home] - lane == row_of[home], 1.0, 0.0), own[home])
        before.append(list(own))
        scale = None
        for p in range(8):
            inverse = 1.0 / spread(diag[p], p)
            scale = inverse if scale is None else jnp.where(row == p, inverse, scale)
            factor = jnp.where(row == p, 0.0, diag[p] * inverse)
            if more:
                low_factor = low[p] * inverse
            for j in range(p + 1, 8):
                entry = spread(diag[j], p)
                diag[j] = diag[j] - factor * entry
                if more:
                    low[j] = low[j] - low_factor * entry
            if more:
                for j in range(8):
                    ahead[j] = ahead[j] - low_factor * spread(low[p], j)
            for k in range(len(own)):
                own[k] = own[k] - across(factor, k) * spread(own[k], p)
            for _ in range(-(-len(pending) // (8 - p))):
                q, *rest = pending.pop(0)
                update(q, *rest)
                cols[q] = columns(q, s)
        solved = [tile * across(scale, k) for k, tile in enumerate(own)]
        after.append(solved)
        for q in range(s + 1, n):
            if q < s + 3:
                update(q, s, cols[q], solved)
            else:
                pending.append((q, s, cols[q], solved))
        if more:
            diag = ahead
            if s + 2 < n:
                cols[s + 2] = columns(s + 2, s + 1)
        if jobs:
            jobs.pop(0)()

    def whole(parts):
        return jnp.concatenate([jnp.concatenate(g, axis=1) for g in parts], axis=0)

    return whole(before), whole(after)


def factorize(a, panel, jobs=()):
    n, m = a.shape
    jobs = list(jobs)
    slabs = [a[i : i + panel] for i in range(0, n, panel)]
    lower, scaled = [], []
    for p in range(len(slabs)):
        lo = p * panel
        w = slabs[p]
        groups = [[w[i : i + 8, t : min(t + lanes, m)] for t in range(0, m, lanes)] for i in range(0, panel, 8)]
        g, r = sweep_panel(groups, lo, jobs)
        lane = lax.broadcasted_iota(jnp.int32, (panel, m), 1)
        row = lax.broadcasted_iota(jnp.int32, (panel, m), 0)
        here = (lane >= lo) & (lane < lo + panel)
        ahead = lane >= lo + row // 8 * 8 + 8
        inner = jnp.where(here & ahead, 0.0, r)
        for q in range(p + 1, len(slabs)):
            slabs[q] = jnp.where(here, 0.0, slabs[q]) - mm_tn(g[:, q * panel : (q + 1) * panel], inner)
        drop = ahead & (lane < n)
        lower.append(jnp.where(drop, 0.0, g))
        scaled.append(jnp.where(drop, 0.0, r))
    for job in jobs:
        job()
    return jnp.concatenate(lower, axis=0), jnp.concatenate(scaled, axis=0)


def pack_symmetric(m):
    third = m.shape[0] // 3
    one, two, three = [slice(i * third, (i + 1) * third) for i in range(3)]
    row = lax.broadcasted_iota(jnp.int32, (third, third), 0)
    col = lax.broadcasted_iota(jnp.int32, (third, third), 1)
    second = m[two, two]
    last = m[three, three]
    diagonal = jnp.sum(jnp.where(row == col, second, 0.0), axis=0, keepdims=True)
    tail = jnp.concatenate([diagonal, jnp.zeros((1, lanes - third), jnp.float32)], axis=1)
    parts = [
        jnp.concatenate([jnp.where(row >= col, m[one, one], second), m[one, two]], axis=1),
        jnp.concatenate([m[one, three], m[two, three]], axis=1),
        jnp.concatenate([last[: third // 2], last[third // 2 :]], axis=1),
        jnp.concatenate([tail, jnp.zeros((7, lanes), jnp.float32)], axis=0),
    ]
    return jnp.concatenate(parts, axis=0)


def unpack_symmetric(p):
    third = lanes // 2
    row = lax.broadcasted_iota(jnp.int32, (third, third), 0)
    col = lax.broadcasted_iota(jnp.int32, (third, third), 1)
    shared, upper = p[:third, :third], p[:third, third:]
    turned = shared.T
    right, mid = p[third : 2 * third, :third], p[third : 2 * third, third:]
    start = 2 * third
    last = p[start : start + third // 2]
    last = jnp.concatenate([last[:, :third], last[:, third:]], axis=0)
    tail = start + third // 2
    first = jnp.where(row >= col, shared, turned)
    second = jnp.where(row == col, p[tail : tail + 1, :third], jnp.where(row < col, shared, turned))
    rows = [
        jnp.concatenate([first, upper, right], axis=1),
        jnp.concatenate([upper.T, second, mid], axis=1),
        jnp.concatenate([right.T, mid.T, last], axis=1),
    ]
    return jnp.concatenate(rows, axis=0)


def with_rhs(packed, f):
    size = packed.shape[0]
    row = lax.broadcasted_iota(jnp.int32, (8, lanes), 0)
    return jnp.concatenate([packed[: size - 8], jnp.where(row == 0, packed[size - 8 :], from_row(f))], axis=0)


def pack_full(m):
    half = m.shape[0] // 2
    tail = jnp.concatenate([m[:half, lanes:], m[half:, lanes:]], axis=1)
    return jnp.concatenate([m[:, :lanes], tail], axis=0)


def unpack_full(p):
    n = p.shape[0] * 2 // 3
    tail = p[n:]
    rest = jnp.concatenate([tail[:, : lanes // 2], tail[:, lanes // 2 :]], axis=0)
    return jnp.concatenate([p[:n], rest], axis=1)


def to_row(f):
    return jnp.concatenate([f[i : i + 1] for i in range(1, 4)], axis=1)


def from_row(row):
    parts = [row[:, i * lanes : (i + 1) * lanes] for i in range(3)]
    zeros = jnp.zeros((4, lanes), jnp.float32)
    return jnp.concatenate([zeros[:1], *parts, zeros], axis=0)


def leaf_kernel(where_ref, after_this_ref, state_ref, source_ref, rate_ref, jac_ref, lift_ref, before_ref, after_ref, sides_ref, f_ref):
    seps = lift_ref.shape[0]
    rows = rate_ref.shape[0]
    width = rate_ref.shape[1]
    chans = jac_ref.shape[0]
    lane = lax.broadcasted_iota(jnp.int32, (8, width), 1)
    where = where_ref[:, :1].astype(jnp.int32)
    lift = []
    for i in range(rows):
        own = lift_ref[:, i, :]
        own = jnp.concatenate([own, jnp.zeros((8 - seps, width), jnp.float32)], axis=0)
        lift.append(own + jnp.where(where == lane + i * width, 1.0, 0.0))
    zero = jnp.zeros((8, width), jnp.float32)
    mixed = []
    for i in range(rows):
        own = lift[i]
        around = (lift[i - 1] if i > 0 else zero) + (lift[i + 1] if i + 1 < rows else zero)
        around = around + jnp.where(lane == 0, 0.0, pltpu.roll(own, 1, 1))
        around = around + jnp.where(lane == width - 1, 0.0, pltpu.roll(own, width - 1, 1))
        mixed.append(jnp.concatenate([0.5 * around - 2.0 * own, own * rate_ref[i : i + 1, :]], axis=0))
    state = jnp.concatenate([state_ref[:, i, :] for i in range(rows)], axis=1)
    source = jnp.concatenate([source_ref[:, i, :] for i in range(rows)], axis=1)
    prod = mm_nt(jnp.concatenate(mixed, axis=1), state, high)
    first = jnp.concatenate([own[:, :1] for own in lift], axis=1)
    last = jnp.concatenate([own[:, width - 1 :] for own in lift], axis=1)
    place = lax.axis_index("axial")
    inside = (place > 0, place < lax.axis_size("axial") - 1)
    before, after = [jnp.where(there, ref[...], 0.0) for there, ref in zip(inside, (before_ref, after_ref))]
    edge = mm_nt(lift[0], before, high) + mm_nt(lift[-1], after, high)
    edge = edge + mm_nt(first, sides_ref[chans:, :], high) + mm_nt(last, sides_ref[:chans, :], high)
    total = prod[:8] + mm_nt(jnp.concatenate(lift, axis=1), source, high)
    total = total - mm(prod[8:], jac_ref[...], high) + 0.5 * edge
    f_ref[...] = from_row(jnp.concatenate([total[i : i + 1] for i in range(seps)], axis=1))


def edges_kernel(state_ref, top_ref, bottom_ref, sides_ref):
    rows, cells = state_ref.shape[1:]
    top_ref[...] = state_ref[:, 0, :]
    bottom_ref[...] = state_ref[:, rows - 1, :]
    left = jnp.concatenate([state_ref[:, i, :1] for i in range(rows)], axis=1)
    right = jnp.concatenate([state_ref[:, i, cells - 1 :] for i in range(rows)], axis=1)
    sides_ref[...] = jnp.concatenate([left, right], axis=0)


def is_upper(level):
    return jnp.bitwise_and(jnp.right_shift(lax.axis_index(everywhere), level), 1) != 0


def order(upper, own, other):
    return jnp.where(upper, other, own), jnp.where(upper, own, other)


def first_kernel(own_ref, other_ref, sep_ref, ss_ref, inv_ref, xt2_ref, where_ref):
    seps = sep_ref.shape[1]
    c_of = lax.broadcasted_iota(jnp.int32, (8, seps), 0)
    own_c = c_of == lax.broadcasted_iota(jnp.int32, (8, seps), 1)
    where = jnp.max(jnp.where(own_c, sep_ref[...], -1), axis=1, keepdims=True)
    where_ref[...] = jnp.broadcast_to(where, (8, lanes)).astype(jnp.float32)
    half = own_ref.shape[0] // 2
    upper = is_upper(0)
    inverse = mm_tn(*factorize(own_ref[half:, half:] + other_ref[half:, half:], half // 3))
    inv_ref[...] = inverse
    _, os2 = order(upper, own_ref[:half, half:], other_ref[:half, half:])
    _, oo2 = order(upper, own_ref[:half, :half], other_ref[:half, :half])
    xt2 = mm(os2, inverse)
    xt2_ref[...] = xt2
    ss_ref[...] = pack_symmetric(oo2 - mm_nt(xt2, os2))


def factor_kernel(own_ref, other_ref, inv_ref):
    inv_ref[...] = mm_tn(*factorize(unpack_symmetric(own_ref[...] + other_ref[...]), inv_ref.shape[0] // 3))


def shared_kernel(level, inv_ref, own_ref, other_ref, ss_ref, xt2_ref):
    upper = is_upper(level)
    size = ss_ref.shape[0]
    _, oo2 = order(upper, own_ref[:size, :], other_ref[:size, :])
    _, os2 = order(upper, own_ref[size:, :], other_ref[size:, :])
    os2 = unpack_full(os2)
    xt2 = mm(os2, inv_ref[...])
    xt2_ref[...] = xt2
    ss_ref[...] = oo2 - pack_symmetric(mm_nt(xt2, os2))


def split_rhs(upper, own_f, other_f):
    own, other = to_row(own_f), to_row(other_f)
    first, second = order(upper, own, other)
    half = own.shape[1] // 2
    return own[:, half:] + other[:, half:], jnp.concatenate([first[:, :half], second[:, :half]], axis=1)


def merge(upper, inv_ref, xt2_ref, os1, os2, own_f, other_f, xt_ref, z_ref):
    half = inv_ref.shape[0]
    shared, outer = split_rhs(upper, own_f, other_f)
    xt = mm(jnp.concatenate([os1, jnp.broadcast_to(shared, (8, half))], axis=0), inv_ref[...])
    xt_ref[:half, :] = xt[:half]
    xt_ref[half:, :] = xt2_ref[...]
    z_ref[...] = xt[half : half + 1]
    both = mm_nt(xt, jnp.concatenate([os1, os2], axis=0))
    return both[:half, :half], -both[:half, half:], outer - both[half : half + 1]


def put_rest(rest_ref, packed, cross, f):
    size = packed.shape[0]
    rest_ref[:size, :] = with_rhs(packed, f)
    rest_ref[size:, :] = pack_full(cross)


def first_rest_kernel(inv_ref, xt2_ref, own_ref, other_ref, after_this_ref, rest_ref, xt_ref):
    half = inv_ref.shape[0]
    upper = is_upper(0)
    os1, os2 = order(upper, own_ref[:half, half:], other_ref[:half, half:])
    oo1, _ = order(upper, own_ref[:half, :half], other_ref[:half, :half])
    xt = mm(os1, inv_ref[...])
    xt_ref[:half, :] = xt
    xt_ref[half:, :] = xt2_ref[...]
    both = mm_nt(xt, jnp.concatenate([os1, os2], axis=0))
    packed = pack_symmetric(oo1 - both[:, :half])
    rest_ref[: packed.shape[0], :] = packed
    rest_ref[packed.shape[0] :, :] = pack_full(-both[:, half:])


def first_rhs_kernel(inv_ref, xt_ref, own_f_ref, other_f_ref, part_ref, rest_ref, z_ref):
    half = inv_ref.shape[0]
    size = rest_ref.shape[0] - half * 3 // 2
    shared, outer = split_rhs(is_upper(0), own_f_ref[...], other_f_ref[...])
    shared = jnp.broadcast_to(shared, (8, half))
    z_ref[...] = mm(shared, inv_ref[...])[:1]
    rest_ref[:size, :] = with_rhs(part_ref[:size, :], outer - mm_nt(shared, xt_ref[...])[:1])
    rest_ref[size:, :] = part_ref[size:, :]


def unpacked(upper, own_ref, other_ref, half):
    size = own_ref.shape[0] - half * 3 // 2
    oo1, oo2 = order(upper, own_ref[:size, :], other_ref[:size, :])
    os1, os2 = order(upper, own_ref[size:, :], other_ref[size:, :])
    return os1, os2, oo1, oo2, own_ref[size - 8 : size, :], other_ref[size - 8 : size, :]


def rest_kernel(level, inv_ref, xt2_ref, own_ref, other_ref, rest_ref, xt_ref, z_ref):
    upper = is_upper(level)
    os1, os2, oo1, _, own_f, other_f = unpacked(upper, own_ref, other_ref, inv_ref.shape[0])
    less, cross, f = merge(
        upper, inv_ref, xt2_ref, unpack_full(os1), unpack_full(os2), own_f, other_f, xt_ref, z_ref
    )
    put_rest(rest_ref, oo1 - pack_symmetric(less), cross, f)


def end_kernel(level, inv_ref, own_ref, other_ref, t_ref, xt_ref, z_ref, end_v_ref, end_r_ref, work_ref):
    half = inv_ref.shape[0]
    upper = is_upper(level)
    os1, os2, oo1, oo2, own_f, other_f = unpacked(upper, own_ref, other_ref, half)
    os1 = unpack_full(os1)
    xt1 = mm(os1, inv_ref[...])
    xt_ref[:half, :] = xt1
    piece = half // 3
    os2 = unpack_full(os2)
    done = {}

    def products(i):
        rows = slice(i * piece, (i + 1) * piece)
        xt_ref[half + i * piece : half + (i + 1) * piece, :] = mm(os2[rows], inv_ref[...])

    def crosses(i):
        rows = slice(i * piece, (i + 1) * piece)
        work_ref[rows, :] = mm_nt(os2[rows], xt_ref[...])

    def right():
        shared, outer = split_rhs(upper, own_f, other_f)
        z = mm(jnp.broadcast_to(shared, (8, half)), inv_ref[...])
        z_ref[...] = z[:1]
        done["f"] = outer - mm_nt(z, jnp.concatenate([os1, os2], axis=0))[:1]

    jobs = [functools.partial(products, i) for i in range(3)] + [functools.partial(crosses, i) for i in range(3)]
    g, r = factorize(unpack_symmetric(oo1) - mm_nt(xt1, os1), half // 2, jobs + [right])
    end_r_ref[...] = r
    f = done["f"]
    stacked = jnp.concatenate([-work_ref[:, :half], jnp.broadcast_to(f[:, :half], (8, half))], axis=0)
    vu = mm_nt(stacked, jnp.concatenate([g, r], axis=0))
    end_v_ref[...] = vu[:, :half]
    lost = mm_nt(vu[:, half:], vu[:half, :half])
    g_row = jnp.concatenate([f[:, half:] - lost[half : half + 1], jnp.zeros((1, half), jnp.float32)], axis=1)
    t_ref[...] = with_rhs(oo2 - pack_symmetric(work_ref[:, half:] + lost[:half]), g_row)


def compose_kernel(levels, end_v_ref, end_r_ref, *refs):
    half = end_r_ref.shape[0]
    out_ref = refs[-1]
    row = lax.broadcasted_iota(jnp.int32, (half + 8, half), 0)
    col = lax.broadcasted_iota(jnp.int32, (half + 8, half), 1)
    outer = mm(jnp.where(row < half, -end_v_ref[...], end_v_ref[...]), end_r_ref[...])
    answer = jnp.concatenate([outer, jnp.where(row == col, 1.0, 0.0)], axis=1)
    for level in reversed(range(levels)):
        xt_ref, z_ref = refs[2 * level : 2 * level + 2]
        inner = jnp.where(row >= half, z_ref[...], 0.0) - mm(answer, xt_ref[...])
        outer = jnp.where(is_upper(level), answer[:, half:], answer[:, :half])
        answer = jnp.concatenate([outer, inner], axis=1)
    out_ref[...] = answer


def solve_kernel(own_ref, other_ref, map_ref, out_ref):
    half = map_ref.shape[0] - 8
    width = map_ref.shape[1]
    total = own_ref[...] + other_ref[...]
    right = jnp.broadcast_to(to_row(total[-8:])[:, :half], (8, half)).T
    pad = jnp.zeros((half, lanes - half % lanes - 8), jnp.float32)
    g, r = factorize(jnp.concatenate([unpack_symmetric(total), right, pad], axis=1), half // 2)
    shared = jnp.sum(g[:, half : half + 1] * r[:, :half], axis=0, keepdims=True)
    shared = jnp.broadcast_to(shared, (8, half)).T[:, :1]
    parts = jnp.broadcast_to(shared, (half, width)) * map_ref[:half, :]
    out_ref[...] = jnp.sum(parts, axis=0, keepdims=True) + map_ref[half : half + 1, :]


vmem = pl.BlockSpec(memory_space=pltpu.VMEM)


def call(kernel, name, shapes, micros, *operands, scratch=()):
    outs = tuple(jax.ShapeDtypeStruct(s, jnp.float32) for s in shapes)
    single = len(outs) == 1
    return pl.pallas_call(
        kernel,
        out_shape=outs[0] if single else outs,
        in_specs=[vmem] * len(operands),
        out_specs=vmem if single else tuple(vmem for _ in outs),
        scratch_shapes=[pltpu.VMEM(shape, jnp.float32) for shape in scratch],
        compiler_params=pltpu.CompilerParams(vmem_limit_bytes=32 << 20),
        cost_estimate=pl.CostEstimate(flops=int(micros * 1e9), bytes_accessed=0, transcendentals=0),
        name=name,
    )(*operands)


def partner(array, level):
    count = lax.axis_size(everywhere)
    return lax.ppermute(array, everywhere, [(i, i ^ 1 << level) for i in range(count)])


def halos(state):
    chans, rows, cells = state.shape
    axial, azim = lax.axis_size("axial"), lax.axis_size("azim")
    shapes = [(chans, cells), (chans, cells), (2 * chans, rows)]
    top, bottom, sides = call(edges_kernel, "edges", shapes, 0.5, state)
    up = [(i, (i + 1) % axial) for i in range(axial)]
    before = lax.ppermute(bottom, "axial", up)
    after = lax.ppermute(top, "axial", [(j, i) for i, j in up])
    around = [(i, (i + 1) % azim) for i in range(azim)]
    if azim == 2:
        sides = lax.ppermute(sides, "azim", around)
    else:
        left = lax.ppermute(sides[chans:], "azim", around)
        right = lax.ppermute(sides[:chans], "azim", [(j, i) for i, j in around])
        sides = jnp.concatenate([right, left], axis=0)
    return before, after, sides


def body(adjoint_state, adjoint_source, reaction_rate, jacobian, lifting, separator, leaf_schur):
    chans, rows, cells = adjoint_state.shape[1:]
    width = leaf_schur.shape[-1]
    half = width // 2
    full = half * 3 // 2
    levels = lax.axis_size(everywhere).bit_length() - 1
    packed = half * 5 // 6 + 8
    rest_shapes = [(packed + full, lanes), (width, half), (1, half)]
    shared_shapes = [(packed, lanes), (half, half)]

    schur = leaf_schur.reshape(width, width)
    other_schur = partner(schur, 0)
    state = adjoint_state.reshape(chans, rows, cells)
    edges = halos(state)
    ss, inverse, xt2, where = call(
        first_kernel,
        "factor_0",
        [*shared_shapes, (half, half), (8, lanes)],
        8.0,
        schur,
        other_schur,
        separator.reshape(1, -1),
    )
    other_ss = partner(ss, 1)
    f = call(
        leaf_kernel,
        "leaf_rhs",
        [(8, lanes)],
        2.3,
        where,
        ss,
        state,
        adjoint_source.reshape(chans, rows, cells),
        reaction_rate.reshape(rows, cells),
        jacobian.reshape(chans, chans),
        lifting.reshape(-1, rows, cells),
        *edges,
    )
    part, xt = call(first_rest_kernel, "rest_0", rest_shapes[:2], 1.0, inverse, xt2, schur, other_schur, f)
    rest, z = call(
        first_rhs_kernel, "rest_rhs_0", rest_shapes[::2], 0.05, inverse, xt, f, partner(f, 0), part
    )
    other_rest = partner(rest, 1)
    saved = [xt, z]
    for level in range(1, levels - 1):
        inverse = call(factor_kernel, f"factor_{level}", [(half, half)], 6.5, ss, other_ss)
        operands = (rest, other_rest)
        if level < levels - 2:
            ss, xt2 = call(
                functools.partial(shared_kernel, level), f"shared_{level}", shared_shapes, 1.5, inverse, *operands
            )
            other_ss = partner(ss, level + 1)
            rest, xt, z = call(
                functools.partial(rest_kernel, level), f"rest_{level}", rest_shapes, 0.05, inverse, xt2, *operands
            )
            other_rest = partner(rest, level + 1)
        else:
            end, xt, z, end_v, end_r = call(
                functools.partial(end_kernel, level),
                f"end_{level}",
                [(packed, lanes), (width, half), (1, half), (half + 8, half), (half, half)],
                9.5,
                inverse,
                *operands,
                scratch=[(half, width)],
            )
        saved += [xt, z]
    other_end = partner(end, levels - 1)
    composed = call(
        functools.partial(compose_kernel, levels - 1), "compose", [(half + 8, width)], 3.7, end_v, end_r, *saved
    )
    answer = call(solve_kernel, "solve", [(1, width)], 7.0, end, other_end, composed)
    return answer.reshape(1, 1, 1, width)


def solution(mesh):
    in_specs = (
        P("bank", None, "axial", "azim"),
        P("bank", None, "axial", "azim"),
        P("bank", "axial", "azim"),
        P("bank", None, None),
        P("bank", None, "axial", "azim"),
        P("axial", "azim", "bank", None),
        P("axial", "azim", "bank", None, None),
    )
    out_specs = P("axial", "azim", "bank", None)
    return jax.shard_map(body, mesh=mesh, in_specs=in_specs, out_specs=out_specs, check_vma=False)
```

```python
import functools

import jax
import jax.numpy as jnp
from jax import lax
from jax.experimental import pallas as pl
from jax.experimental.pallas import tpu as pltpu
from jax.sharding import PartitionSpec as P

highest = lax.Precision.HIGHEST
high = lax.Precision.HIGH
everywhere = ("axial", "azim", "bank")
lanes = 128


def mm(a, b, precision=highest):
    return jnp.dot(a, b, precision=precision, preferred_element_type=jnp.float32)


def mm_nt(a, b, precision=highest):
    dims = (((1,), (1,)), ((), ()))
    return lax.dot_general(a, b, dims, precision=precision, preferred_element_type=jnp.float32)


def mm_tn(a, b, precision=highest):
    dims = (((0,), (0,)), ((), ()))
    return lax.dot_general(a, b, dims, precision=precision, preferred_element_type=jnp.float32)


def sweep_panel(groups, first, jobs):
    n = len(groups)
    groups = [list(g) for g in groups]
    widths = [t.shape[1] for t in groups[0]]
    row = lax.broadcasted_iota(jnp.int32, (8, lanes), 0)
    lane_of = [lax.broadcasted_iota(jnp.int32, (8, w), 1) for w in widths]
    row_of = [lax.broadcasted_iota(jnp.int32, (8, w), 0) for w in widths]

    def columns(q, s):
        tile, lane = divmod(first + 8 * s, lanes)
        return [jnp.broadcast_to(groups[q][tile][:, lane + m : lane + m + 1], (8, lanes)) for m in range(8)]

    def across(column, tile):
        return column if widths[tile] == lanes else column[:, : widths[tile]]

    def spread(value, i):
        return jnp.broadcast_to(value[i : i + 1], value.shape)

    def inside(s):
        tile, lane = divmod(first + 8 * s, lanes)
        return tile, lane, (lane_of[tile] >= lane) & (lane_of[tile] < lane + 8)

    def update(q, s, cols, solved):
        home, _, here = inside(s)
        new = []
        for k, tile in enumerate(groups[q]):
            value = jnp.where(here, 0.0, tile) if k == home else tile
            for m in range(8):
                value = value - across(cols[m], k) * spread(solved[k], m)
            new.append(value)
        groups[q] = new

    diag = columns(0, 0)
    cols = {q: columns(q, 0) for q in range(1, n)}
    pending, before, after = [], [], []
    for s in range(n):
        more = s + 1 < n
        if more:
            low, ahead = list(cols[s + 1]), columns(s + 1, s + 1)
        home, lane, here = inside(s)
        own = list(groups[s])
        own[home] = jnp.where(here, jnp.where(lane_of[home] - lane == row_of[home], 1.0, 0.0), own[home])
        before.append(list(own))
        scale = None
        for p in range(8):
            inverse = 1.0 / spread(diag[p], p)
            scale = inverse if scale is None else jnp.where(row == p, inverse, scale)
            factor = jnp.where(row == p, 0.0, diag[p] * inverse)
            if more:
                low_factor = low[p] * inverse
            for j in range(p + 1, 8):
                entry = spread(diag[j], p)
                diag[j] = diag[j] - factor * entry
                if more:
                    low[j] = low[j] - low_factor * entry
            if more:
                for j in range(8):
                    ahead[j] = ahead[j] - low_factor * spread(low[p], j)
            for k in range(len(own)):
                own[k] = own[k] - across(factor, k) * spread(own[k], p)
            for _ in range(-(-len(pending) // (8 - p))):
                q, *rest = pending.pop(0)
                update(q, *rest)
                cols[q] = columns(q, s)
        solved = [tile * across(scale, k) for k, tile in enumerate(own)]
        after.append(solved)
        for q in range(s + 1, n):
            if q < s + 3:
                update(q, s, cols[q], solved)
            else:
                pending.append((q, s, cols[q], solved))
        if more:
            diag = ahead
            if s + 2 < n:
                cols[s + 2] = columns(s + 2, s + 1)
        if jobs:
            jobs.pop(0)()

    def whole(parts):
        return jnp.concatenate([jnp.concatenate(g, axis=1) for g in parts], axis=0)

    return whole(before), whole(after)


def factorize(a, panel, jobs=()):
    n, m = a.shape
    jobs = list(jobs)
    slabs = [a[i : i + panel] for i in range(0, n, panel)]
    lower, scaled = [], []
    for p in range(len(slabs)):
        lo = p * panel
        w = slabs[p]
        groups = [[w[i : i + 8, t : min(t + lanes, m)] for t in range(0, m, lanes)] for i in range(0, panel, 8)]
        g, r = sweep_panel(groups, lo, jobs)
        lane = lax.broadcasted_iota(jnp.int32, (panel, m), 1)
        row = lax.broadcasted_iota(jnp.int32, (panel, m), 0)
        here = (lane >= lo) & (lane < lo + panel)
        ahead = lane >= lo + row // 8 * 8 + 8
        inner = jnp.where(here & ahead, 0.0, r)
        for q in range(p + 1, len(slabs)):
            slabs[q] = jnp.where(here, 0.0, slabs[q]) - mm_tn(g[:, q * panel : (q + 1) * panel], inner)
        drop = ahead & (lane < n)
        lower.append(jnp.where(drop, 0.0, g))
        scaled.append(jnp.where(drop, 0.0, r))
    for job in jobs:
        job()
    return jnp.concatenate(lower, axis=0), jnp.concatenate(scaled, axis=0)


def pack_symmetric(m):
    third = m.shape[0] // 3
    one, two, three = [slice(i * third, (i + 1) * third) for i in range(3)]
    row = lax.broadcasted_iota(jnp.int32, (third, third), 0)
    col = lax.broadcasted_iota(jnp.int32, (third, third), 1)
    second = m[two, two]
    last = m[three, three]
    diagonal = jnp.sum(jnp.where(row == col, second, 0.0), axis=0, keepdims=True)
    tail = jnp.concatenate([diagonal, jnp.zeros((1, lanes - third), jnp.float32)], axis=1)
    parts = [
        jnp.concatenate([jnp.where(row >= col, m[one, one], second), m[one, two]], axis=1),
        jnp.concatenate([m[one, three], m[two, three]], axis=1),
        jnp.concatenate([last[: third // 2], last[third // 2 :]], axis=1),
        jnp.concatenate([tail, jnp.zeros((7, lanes), jnp.float32)], axis=0),
    ]
    return jnp.concatenate(parts, axis=0)


def unpack_symmetric(p):
    third = lanes // 2
    row = lax.broadcasted_iota(jnp.int32, (third, third), 0)
    col = lax.broadcasted_iota(jnp.int32, (third, third), 1)
    shared, upper = p[:third, :third], p[:third, third:]
    turned = shared.T
    right, mid = p[third : 2 * third, :third], p[third : 2 * third, third:]
    start = 2 * third
    last = p[start : start + third // 2]
    last = jnp.concatenate([last[:, :third], last[:, third:]], axis=0)
    tail = start + third // 2
    first = jnp.where(row >= col, shared, turned)
    second = jnp.where(row == col, p[tail : tail + 1, :third], jnp.where(row < col, shared, turned))
    rows = [
        jnp.concatenate([first, upper, right], axis=1),
        jnp.concatenate([upper.T, second, mid], axis=1),
        jnp.concatenate([right.T, mid.T, last], axis=1),
    ]
    return jnp.concatenate(rows, axis=0)


def with_rhs(packed, f):
    size = packed.shape[0]
    row = lax.broadcasted_iota(jnp.int32, (8, lanes), 0)
    return jnp.concatenate([packed[: size - 8], jnp.where(row == 0, packed[size - 8 :], from_row(f))], axis=0)


def pack_full(m):
    half = m.shape[0] // 2
    tail = jnp.concatenate([m[:half, lanes:], m[half:, lanes:]], axis=1)
    return jnp.concatenate([m[:, :lanes], tail], axis=0)


def unpack_full(p):
    n = p.shape[0] * 2 // 3
    tail = p[n:]
    rest = jnp.concatenate([tail[:, : lanes // 2], tail[:, lanes // 2 :]], axis=0)
    return jnp.concatenate([p[:n], rest], axis=1)


def to_row(f):
    return jnp.concatenate([f[i : i + 1] for i in range(1, 4)], axis=1)


def from_row(row):
    parts = [row[:, i * lanes : (i + 1) * lanes] for i in range(3)]
    zeros = jnp.zeros((4, lanes), jnp.float32)
    return jnp.concatenate([zeros[:1], *parts, zeros], axis=0)


def leaf_kernel(where_ref, after_this_ref, state_ref, source_ref, rate_ref, jac_ref, lift_ref, before_ref, after_ref, sides_ref, f_ref):
    seps = lift_ref.shape[0]
    rows = rate_ref.shape[0]
    width = rate_ref.shape[1]
    chans = jac_ref.shape[0]
    lane = lax.broadcasted_iota(jnp.int32, (8, width), 1)
    where = where_ref[:, :1].astype(jnp.int32)
    lift = []
    for i in range(rows):
        own = lift_ref[:, i, :]
        own = jnp.concatenate([own, jnp.zeros((8 - seps, width), jnp.float32)], axis=0)
        lift.append(own + jnp.where(where == lane + i * width, 1.0, 0.0))
    zero = jnp.zeros((8, width), jnp.float32)
    mixed = []
    for i in range(rows):
        own = lift[i]
        around = (lift[i - 1] if i > 0 else zero) + (lift[i + 1] if i + 1 < rows else zero)
        around = around + jnp.where(lane == 0, 0.0, pltpu.roll(own, 1, 1))
        around = around + jnp.where(lane == width - 1, 0.0, pltpu.roll(own, width - 1, 1))
        mixed.append(jnp.concatenate([0.5 * around - 2.0 * own, own * rate_ref[i : i + 1, :]], axis=0))
    state = jnp.concatenate([state_ref[:, i, :] for i in range(rows)], axis=1)
    source = jnp.concatenate([source_ref[:, i, :] for i in range(rows)], axis=1)
    prod = mm_nt(jnp.concatenate(mixed, axis=1), state, high)
    first = jnp.concatenate([own[:, :1] for own in lift], axis=1)
    last = jnp.concatenate([own[:, width - 1 :] for own in lift], axis=1)
    place = lax.axis_index("axial")
    inside = (place > 0, place < lax.axis_size("axial") - 1)
    before, after = [jnp.where(there, ref[...], 0.0) for there, ref in zip(inside, (before_ref, after_ref))]
    edge = mm_nt(lift[0], before, high) + mm_nt(lift[-1], after, high)
    edge = edge + mm_nt(first, sides_ref[chans:, :], high) + mm_nt(last, sides_ref[:chans, :], high)
    total = prod[:8] + mm_nt(jnp.concatenate(lift, axis=1), source, high)
    total = total - mm(prod[8:], jac_ref[...], high) + 0.5 * edge
    f_ref[...] = from_row(jnp.concatenate([total[i : i + 1] for i in range(seps)], axis=1))


def edges_kernel(state_ref, top_ref, bottom_ref, sides_ref):
    rows, cells = state_ref.shape[1:]
    top_ref[...] = state_ref[:, 0, :]
    bottom_ref[...] = state_ref[:, rows - 1, :]
    left = jnp.concatenate([state_ref[:, i, :1] for i in range(rows)], axis=1)
    right = jnp.concatenate([state_ref[:, i, cells - 1 :] for i in range(rows)], axis=1)
    sides_ref[...] = jnp.concatenate([left, right], axis=0)


def is_upper(level):
    return jnp.bitwise_and(jnp.right_shift(lax.axis_index(everywhere), level), 1) != 0


def order(upper, own, other):
    return jnp.where(upper, other, own), jnp.where(upper, own, other)


def first_kernel(own_ref, other_ref, sep_ref, ss_ref, inv_ref, xt2_ref, where_ref):
    seps = sep_ref.shape[1]
    c_of = lax.broadcasted_iota(jnp.int32, (8, seps), 0)
    own_c = c_of == lax.broadcasted_iota(jnp.int32, (8, seps), 1)
    where = jnp.max(jnp.where(own_c, sep_ref[...], -1), axis=1, keepdims=True)
    where_ref[...] = jnp.broadcast_to(where, (8, lanes)).astype(jnp.float32)
    half = own_ref.shape[0] // 2
    upper = is_upper(0)
    inverse = mm_tn(*factorize(own_ref[half:, half:] + other_ref[half:, half:], half // 3))
    inv_ref[...] = inverse
    _, os2 = order(upper, own_ref[:half, half:], other_ref[:half, half:])
    _, oo2 = order(upper, own_ref[:half, :half], other_ref[:half, :half])
    xt2 = mm(os2, inverse)
    xt2_ref[...] = xt2
    ss_ref[...] = pack_symmetric(oo2 - mm_nt(xt2, os2))


def factor_kernel(own_ref, other_ref, *refs):
    g_ref, r_ref = refs[-2:]
    g_ref[...], r_ref[...] = factorize(unpack_symmetric(own_ref[...] + other_ref[...]), g_ref.shape[0] // 2)


def inverse_kernel(g_ref, r_ref, *refs):
    inv_ref = refs[-1]
    inv_ref[...] = mm_tn(g_ref[...], r_ref[...])


def shared_kernel(level, inv_ref, own_ref, other_ref, *refs):
    ss_ref, xt2_ref = refs[-2:]
    upper = is_upper(level)
    size = ss_ref.shape[0]
    _, oo2 = order(upper, own_ref[:size, :], other_ref[:size, :])
    _, os2 = order(upper, own_ref[size:, :], other_ref[size:, :])
    os2 = unpack_full(os2)
    xt2 = mm(os2, inv_ref[...])
    xt2_ref[...] = xt2
    ss_ref[...] = oo2 - pack_symmetric(mm_nt(xt2, os2))


def split_rhs(upper, own_f, other_f):
    own, other = to_row(own_f), to_row(other_f)
    first, second = order(upper, own, other)
    half = own.shape[1] // 2
    return own[:, half:] + other[:, half:], jnp.concatenate([first[:, :half], second[:, :half]], axis=1)


def merge(upper, inv_ref, xt2_ref, os1, os2, own_f, other_f, xt_ref, z_ref):
    half = inv_ref.shape[0]
    shared, outer = split_rhs(upper, own_f, other_f)
    xt = mm(jnp.concatenate([os1, jnp.broadcast_to(shared, (8, half))], axis=0), inv_ref[...])
    xt_ref[:half, :] = xt[:half]
    xt_ref[half:, :] = xt2_ref[...]
    z_ref[...] = xt[half : half + 1]
    both = mm_nt(xt, jnp.concatenate([os1, os2], axis=0))
    return both[:half, :half], -both[:half, half:], outer - both[half : half + 1]


def put_rest(rest_ref, packed, cross, f):
    size = packed.shape[0]
    rest_ref[:size, :] = with_rhs(packed, f)
    rest_ref[size:, :] = pack_full(cross)


def first_rest_kernel(inv_ref, xt2_ref, own_ref, other_ref, rest_ref, xt_ref):
    half = inv_ref.shape[0]
    upper = is_upper(0)
    os1, os2 = order(upper, own_ref[:half, half:], other_ref[:half, half:])
    oo1, _ = order(upper, own_ref[:half, :half], other_ref[:half, :half])
    xt = mm(os1, inv_ref[...])
    xt_ref[:half, :] = xt
    xt_ref[half:, :] = xt2_ref[...]
    both = mm_nt(xt, jnp.concatenate([os1, os2], axis=0))
    packed = pack_symmetric(oo1 - both[:, :half])
    rest_ref[: packed.shape[0], :] = packed
    rest_ref[packed.shape[0] :, :] = pack_full(-both[:, half:])


def first_rhs_kernel(inv_ref, xt_ref, own_f_ref, other_f_ref, f_ref, z_ref):
    half = inv_ref.shape[0]
    shared, outer = split_rhs(is_upper(0), own_f_ref[...], other_f_ref[...])
    shared = jnp.broadcast_to(shared, (8, half))
    z_ref[...] = mm(shared, inv_ref[...])[:1]
    f_ref[...] = from_row(outer - mm_nt(shared, xt_ref[...])[:1])


def unpacked(upper, own_ref, other_ref, half):
    size = own_ref.shape[0] - half * 3 // 2
    oo1, oo2 = order(upper, own_ref[:size, :], other_ref[:size, :])
    os1, os2 = order(upper, own_ref[size:, :], other_ref[size:, :])
    return os1, os2, oo1, oo2, own_ref[size - 8 : size, :], other_ref[size - 8 : size, :]


def rest_kernel(level, inv_ref, xt2_ref, own_ref, other_ref, *refs):
    *sides, rest_ref, xt_ref, z_ref = refs
    upper = is_upper(level)
    os1, os2, oo1, _, own_f, other_f = unpacked(upper, own_ref, other_ref, inv_ref.shape[0])
    if sides:
        own_f, other_f = [side[...] for side in sides]
    less, cross, f = merge(
        upper, inv_ref, xt2_ref, unpack_full(os1), unpack_full(os2), own_f, other_f, xt_ref, z_ref
    )
    put_rest(rest_ref, oo1 - pack_symmetric(less), cross, f)


def end_kernel(level, inv_ref, own_ref, other_ref, t_ref, xt_ref, z_ref, end_v_ref, end_r_ref, work_ref):
    half = inv_ref.shape[0]
    upper = is_upper(level)
    os1, os2, oo1, oo2, own_f, other_f = unpacked(upper, own_ref, other_ref, half)
    os1 = unpack_full(os1)
    xt1 = mm(os1, inv_ref[...])
    xt_ref[:half, :] = xt1
    piece = half // 3
    os2 = unpack_full(os2)
    done = {}

    def products(i):
        rows = slice(i * piece, (i + 1) * piece)
        xt_ref[half + i * piece : half + (i + 1) * piece, :] = mm(os2[rows], inv_ref[...])

    def crosses(i):
        rows = slice(i * piece, (i + 1) * piece)
        work_ref[rows, :] = mm_nt(os2[rows], xt_ref[...])

    def right():
        shared, outer = split_rhs(upper, own_f, other_f)
        z = mm(jnp.broadcast_to(shared, (8, half)), inv_ref[...])
        z_ref[...] = z[:1]
        done["f"] = outer - mm_nt(z, jnp.concatenate([os1, os2], axis=0))[:1]

    jobs = [functools.partial(products, i) for i in range(3)] + [functools.partial(crosses, i) for i in range(3)]
    g, r = factorize(unpack_symmetric(oo1) - mm_nt(xt1, os1), half // 2, jobs + [right])
    end_r_ref[...] = r
    f = done["f"]
    stacked = jnp.concatenate([-work_ref[:, :half], jnp.broadcast_to(f[:, :half], (8, half))], axis=0)
    vu = mm_nt(stacked, jnp.concatenate([g, r], axis=0))
    end_v_ref[...] = vu[:, :half]
    lost = mm_nt(vu[:, half:], vu[:half, :half])
    g_row = jnp.concatenate([f[:, half:] - lost[half : half + 1], jnp.zeros((1, half), jnp.float32)], axis=1)
    t_ref[...] = with_rhs(oo2 - pack_symmetric(work_ref[:, half:] + lost[:half]), g_row)


def compose_kernel(levels, end_v_ref, end_r_ref, *refs):
    half = end_r_ref.shape[0]
    out_ref = refs[-1]
    row = lax.broadcasted_iota(jnp.int32, (half + 8, half), 0)
    col = lax.broadcasted_iota(jnp.int32, (half + 8, half), 1)
    outer = mm(jnp.where(row < half, -end_v_ref[...], end_v_ref[...]), end_r_ref[...])
    answer = jnp.concatenate([outer, jnp.where(row == col, 1.0, 0.0)], axis=1)
    for level in reversed(range(levels)):
        xt_ref, z_ref = refs[2 * level : 2 * level + 2]
        inner = jnp.where(row >= half, z_ref[...], 0.0) - mm(answer, xt_ref[...])
        outer = jnp.where(is_upper(level), answer[:, half:], answer[:, :half])
        answer = jnp.concatenate([outer, inner], axis=1)
    out_ref[...] = answer


def solve_kernel(own_ref, other_ref, map_ref, out_ref):
    half = map_ref.shape[0] - 8
    width = map_ref.shape[1]
    total = own_ref[...] + other_ref[...]
    right = jnp.broadcast_to(to_row(total[-8:])[:, :half], (8, half)).T
    pad = jnp.zeros((half, lanes - half % lanes - 8), jnp.float32)
    g, r = factorize(jnp.concatenate([unpack_symmetric(total), right, pad], axis=1), half // 2)
    shared = jnp.sum(g[:, half : half + 1] * r[:, :half], axis=0, keepdims=True)
    shared = jnp.broadcast_to(shared, (8, half)).T[:, :1]
    parts = jnp.broadcast_to(shared, (half, width)) * map_ref[:half, :]
    out_ref[...] = jnp.sum(parts, axis=0, keepdims=True) + map_ref[half : half + 1, :]


vmem = pl.BlockSpec(memory_space=pltpu.VMEM)


def call(kernel, name, shapes, micros, *operands, scratch=()):
    outs = tuple(jax.ShapeDtypeStruct(s, jnp.float32) for s in shapes)
    single = len(outs) == 1
    return pl.pallas_call(
        kernel,
        out_shape=outs[0] if single else outs,
        in_specs=[vmem] * len(operands),
        out_specs=vmem if single else tuple(vmem for _ in outs),
        scratch_shapes=[pltpu.VMEM(shape, jnp.float32) for shape in scratch],
        compiler_params=pltpu.CompilerParams(vmem_limit_bytes=32 << 20),
        cost_estimate=pl.CostEstimate(flops=int(micros * 1e9), bytes_accessed=0, transcendentals=0),
        name=name,
    )(*operands)


def partner(array, level):
    count = lax.axis_size(everywhere)
    return lax.ppermute(array, everywhere, [(i, i ^ 1 << level) for i in range(count)])


def halos(state):
    chans, rows, cells = state.shape
    axial, azim = lax.axis_size("axial"), lax.axis_size("azim")
    shapes = [(chans, cells), (chans, cells), (2 * chans, rows)]
    top, bottom, sides = call(edges_kernel, "edges", shapes, 0.5, state)
    up = [(i, (i + 1) % axial) for i in range(axial)]
    before = lax.ppermute(bottom, "axial", up)
    after = lax.ppermute(top, "axial", [(j, i) for i, j in up])
    around = [(i, (i + 1) % azim) for i in range(azim)]
    if azim == 2:
        sides = lax.ppermute(sides, "azim", around)
    else:
        left = lax.ppermute(sides[chans:], "azim", around)
        right = lax.ppermute(sides[:chans], "azim", [(j, i) for i, j in around])
        sides = jnp.concatenate([right, left], axis=0)
    return before, after, sides


def body(adjoint_state, adjoint_source, reaction_rate, jacobian, lifting, separator, leaf_schur):
    chans, rows, cells = adjoint_state.shape[1:]
    width = leaf_schur.shape[-1]
    half = width // 2
    full = half * 3 // 2
    levels = lax.axis_size(everywhere).bit_length() - 1
    packed = half * 5 // 6 + 8
    rest_shapes = [(packed + full, lanes), (width, half), (1, half)]
    shared_shapes = [(packed, lanes), (half, half)]

    schur = leaf_schur.reshape(width, width)
    other_schur = partner(schur, 0)
    state = adjoint_state.reshape(chans, rows, cells)
    edges = halos(state)
    ss, inverse, xt2, where = call(
        first_kernel,
        "factor_0",
        [*shared_shapes, (half, half), (8, lanes)],
        8.0,
        schur,
        other_schur,
        separator.reshape(1, -1),
    )
    other_ss = partner(ss, 1)
    rest, xt = call(first_rest_kernel, "rest_0", rest_shapes[:2], 0.05, inverse, xt2, schur, other_schur)
    other_rest = partner(rest, 1)
    f = call(
        leaf_kernel,
        "leaf_rhs",
        [(8, lanes)],
        2.3,
        where,
        rest,
        state,
        adjoint_source.reshape(chans, rows, cells),
        reaction_rate.reshape(rows, cells),
        jacobian.reshape(chans, chans),
        lifting.reshape(-1, rows, cells),
        *edges,
    )
    f, z = call(
        first_rhs_kernel, "rest_rhs_0", [(8, lanes), (1, half)], 0.5, inverse, xt, f, partner(f, 0)
    )
    sides = (f, partner(f, 1))
    saved = [xt, z]
    for level in range(1, levels - 1):
        factors = call(factor_kernel, f"factor_{level}", [(half, half), (half, half)], 5.0 if level > 1 else 0.3, ss, other_ss, *sides[:1])
        inverse = call(inverse_kernel, f"inverse_{level}", [(half, half)], 0.5, *factors, *sides[1:])
        operands = (rest, other_rest)
        if level < levels - 2:
            ss, xt2 = call(
                functools.partial(shared_kernel, level),
                f"shared_{level}",
                shared_shapes,
                1.5,
                inverse,
                *operands,
            )
            other_ss = partner(ss, level + 1)
            rest, xt, z = call(
                functools.partial(rest_kernel, level),
                f"rest_{level}",
                rest_shapes,
                0.05,
                inverse,
                xt2,
                *operands,
                *sides,
            )
            other_rest = partner(rest, level + 1)
        else:
            end, xt, z, end_v, end_r = call(
                functools.partial(end_kernel, level),
                f"end_{level}",
                [(packed, lanes), (width, half), (1, half), (half + 8, half), (half, half)],
                9.5,
                inverse,
                *operands,
                scratch=[(half, width)],
            )
        saved += [xt, z]
        sides = ()
    other_end = partner(end, levels - 1)
    composed = call(
        functools.partial(compose_kernel, levels - 1), "compose", [(half + 8, width)], 3.7, end_v, end_r, *saved
    )
    answer = call(solve_kernel, "solve", [(1, width)], 7.0, end, other_end, composed)
    return answer.reshape(1, 1, 1, width)


def solution(mesh):
    in_specs = (
        P("bank", None, "axial", "azim"),
        P("bank", None, "axial", "azim"),
        P("bank", "axial", "azim"),
        P("bank", None, None),
        P("bank", None, "axial", "azim"),
        P("axial", "azim", "bank", None),
        P("axial", "azim", "bank", None, None),
    )
    out_specs = P("axial", "azim", "bank", None)
    return jax.shard_map(body, mesh=mesh, in_specs=in_specs, out_specs=out_specs, check_vma=False)
```
